32 devices in a mesh: section: 8 (over y, x, core), expert: 4 (over z).
Axes of the slice: x: 2, y: 2, z: 4, core: 2. Of those that a mesh axis runs over, the one named last changes fastest.
Arguments:
- activations: bfloat16 [8192, 8192], P('section', 'expert'), may hold values from -12 to 12
- modality: int32 [8192], P('section'), may hold values from 0 to 1
- selected: int32 [8, 256], P('section'), may hold values from 0 to 1023, as said below
- routes: int32 [2048, 1], P('section'), may hold values from 0 to 3, as said below
- norm_gain: float32 [2, 8192], P(None, 'expert'), may hold values from 0.1 to 1.9
- router: float32 [8192], P('expert'), may hold values from -0.0625 to 0.0625
- gate_w: bfloat16 [4, 3072, 8192], P('expert', 'section'), may hold values from -0.0625 to 0.0625
- up_w: bfloat16 [4, 3072, 8192], P('expert', 'section'), may hold values from -0.0625 to 0.0625
- down_w: bfloat16 [4, 3072, 8192], P('expert', 'section'), may hold values from -0.21875 to 0.21875
Outputs:
- block_out: bfloat16 [8192, 8192], P('section', 'expert')
The draws below stay inside these ranges and needn't reach their ends.
Inputs may be any that keep to these rules, and one draw needn't show every extreme that they name: Each row of selected lists 256 different positions in rising order, the first and the last position among them. `routes`: among the 256 rows of one section group no expert is named more than 96 times, and some expert exactly 96 times; the entry for selected[s, j] is below 2 if that token's modality is 0, and 2 or more if it is 1.
All inputs are finite; a program needn't handle non-finite values.
Results may differ from the reference program's by a relative error of at most 0.0075.
Values may be sent and summed in bfloat16 or wider, within the bound.
A program may use at most 128 MiB of HBM per device.

```python
import math
import jax
import jax.numpy as jnp
from jax import lax

D = 8192
FF = 3072
TOK_SECTION = 1024
EXPERTS = 4
SEL_SECTION = 256
CAP = 96
HID_DEV = 384
TOKENS = 8192
N_SECTION = 8


def draw_activations(key, part):
    first, second = jax.random.split(key)
    base = jax.random.normal(first, (TOKENS, D), jnp.float32)
    columns = jnp.arange(D, dtype=jnp.float32) / D
    col_scale = 3.0 ** (columns - 0.5)
    row_scale = jnp.exp(jax.random.uniform(second, (TOKENS, 1), jnp.float32, math.log(0.6), math.log(1.6)))
    return jnp.clip(base * col_scale[None, :] * row_scale, -12.0, 12.0).astype(jnp.bfloat16)


def section_block(block_key):
    sel_key, bias_key, force_key, noise_key, mix_key, kind_key = jax.random.split(block_key, 6)
    order = jax.random.permutation(sel_key, TOK_SECTION).astype(jnp.int32)
    places = jnp.arange(TOK_SECTION, dtype=jnp.int32)
    order = jnp.where(places == 0, -2, order)
    order = jnp.where(places == TOK_SECTION - 1, -1, order)
    chosen = jnp.sort(jnp.argsort(order, stable=True)[:SEL_SECTION].astype(jnp.int32))
    slot_total = EXPERTS * CAP
    bias = jax.random.randint(bias_key, (EXPERTS,), 0, 4).astype(jnp.int32)
    forced = jax.random.randint(force_key, (), 0, EXPERTS).astype(jnp.int32)
    bias = jnp.where(jnp.arange(EXPERTS, dtype=jnp.int32) == forced, 8, bias)
    owners = jnp.arange(slot_total, dtype=jnp.int32) // CAP
    noise = jax.random.randint(noise_key, (slot_total,), 0, 65536).astype(jnp.int32)
    scores = (bias[owners] * 65536 + noise) * slot_total + jnp.arange(slot_total, dtype=jnp.int32)
    taken = jnp.argsort(-scores)[:SEL_SECTION].astype(jnp.int32)
    experts = owners[taken]
    experts = experts[jax.random.permutation(mix_key, SEL_SECTION)].astype(jnp.int32)
    kinds = jax.random.randint(kind_key, (TOK_SECTION,), 0, 2).astype(jnp.int32)
    kinds = kinds.at[chosen].set((experts >= EXPERTS // 2).astype(jnp.int32))
    return (chosen, experts, kinds)


def common_draw(key):
    base = jax.random.fold_in(key, 7321)
    keys = jax.vmap(lambda index: jax.random.fold_in(base, index))(jnp.arange(N_SECTION, dtype=jnp.int32))
    return jax.vmap(section_block)(keys)


def draw_selected(key, part):
    chosen, experts, kinds = common_draw(key)
    return chosen.astype(jnp.int32)


def draw_routes(key, part):
    chosen, experts, kinds = common_draw(key)
    return experts.reshape(N_SECTION * SEL_SECTION, 1).astype(jnp.int32)


def draw_modality(key, part):
    chosen, experts, kinds = common_draw(key)
    return kinds.reshape(TOKENS).astype(jnp.int32)


def level_of(rng, dims, cuts, smallest, top_value):
    factor_of, own = 1.0, jax.random.fold_in(rng, 6)
    for axis_at, blocks in cuts:
        draws = jnp.exp(jax.random.uniform(jax.random.fold_in(own, axis_at), (blocks,), jnp.float32, smallest / len(cuts), top_value / len(cuts)))
        factor_of = factor_of * jnp.repeat(draws, dims[axis_at] // blocks).reshape([-1 if axis == axis_at else 1 for axis in range(len(dims))])
    return factor_of


def normal_values(key, shape, scale, bound, cuts=(), kind=jnp.bfloat16):
    drawn = jax.random.normal(key, shape, jnp.float32) * scale
    if len(cuts) > 0:
        drawn = level_of(key, shape, cuts, -0.22, 0.18) * drawn
    return jnp.clip(drawn, min=-bound, max=bound).astype(kind)


def setup_inputs(seed: int = 0) -> dict:
    streams_of = jax.random.split(jax.random.key(seed), 10)
    return {
        "activations": draw_activations(jax.random.fold_in(streams_of[9], 71), 0),
        "modality": draw_modality(jax.random.fold_in(streams_of[9], 71), 0),
        "selected": draw_selected(jax.random.fold_in(streams_of[9], 71), 0),
        "routes": draw_routes(jax.random.fold_in(streams_of[9], 71), 0),
        "norm_gain": jnp.clip(1.0 + 0.18 * jax.random.normal(streams_of[4], (2, D), jnp.float32), 0.1, 1.9),
        "router": normal_values(streams_of[5], (D,), D ** -0.5, 0.0625, ((0, 4),), jnp.float32),
        "gate_w": normal_values(streams_of[6], (EXPERTS, FF, D), D ** -0.5, 0.0625, ((0, 4), (1, 8))),
        "up_w": normal_values(streams_of[7], (EXPERTS, FF, D), D ** -0.5, 0.0625, ((0, 4), (1, 8))),
        "down_w": normal_values(streams_of[8], (EXPERTS, FF, D), (FF // 4) ** -0.5, 0.21875, ((0, 4), (1, 8))),
    }


EPS = 1e-05

def reference(activations, modality, selected, routes, norm_gain, router, gate_w, up_w, down_w):
    arrived = jnp.roll(activations, TOK_SECTION, axis=0)
    offsets = (jnp.arange(N_SECTION, dtype=jnp.int32) * TOK_SECTION)[:, None]
    picks = (selected + offsets).reshape(-1).astype(jnp.int32)
    picked = arrived[picks].astype(jnp.float32)
    kinds = modality[picks]
    gains = jnp.where(kinds[:, None] == 1, norm_gain[1][None, :], norm_gain[0][None, :])
    scale = lax.rsqrt(lax.optimization_barrier(jnp.sum(picked * picked, axis=1)) / D + EPS)
    normed = (picked * scale[:, None] * gains).astype(jnp.bfloat16)
    score = jax.nn.sigmoid(scale * lax.optimization_barrier(jnp.sum(picked * gains * router[None, :], axis=1)))
    experts = routes[:, 0].reshape(N_SECTION, SEL_SECTION).astype(jnp.int32)
    onehot = (experts[:, :, None] == jnp.arange(EXPERTS, dtype=jnp.int32)[None, None, :]).astype(jnp.int32)
    ranks = jnp.cumsum(onehot, axis=1) - 1
    slot = lax.optimization_barrier(jnp.sum(ranks * onehot, axis=2)).astype(jnp.int32)
    position = (jnp.arange(N_SECTION, dtype=jnp.int32)[:, None] * CAP + slot).reshape(-1).astype(jnp.int32)
    flat_experts = experts.reshape(-1)
    buffers = jnp.zeros((EXPERTS, N_SECTION * CAP, D), jnp.bfloat16).at[flat_experts, position].set(normed)

    def one_expert(items):
        buffer, wgate, wup, wdown = items
        gate = jnp.dot(buffer, wgate.T, preferred_element_type=jnp.float32)
        upper = jnp.dot(buffer, wup.T, preferred_element_type=jnp.float32)
        hidden = (jax.nn.silu(gate) * upper).astype(jnp.bfloat16)
        blocks = hidden.astype(jnp.float32).reshape(N_SECTION * CAP, N_SECTION, HID_DEV)
        weights = wdown.astype(jnp.float32).reshape(N_SECTION, HID_DEV, D)
        parts = jnp.einsum('rbk,bkc->brc', blocks, weights)
        parts = lax.optimization_barrier(parts.astype(jnp.bfloat16)).astype(jnp.float32)
        return lax.optimization_barrier(jnp.sum(parts, axis=0)).astype(jnp.bfloat16)
    expert_out = lax.map(one_expert, (buffers, gate_w, up_w, down_w))
    rows_out = expert_out[flat_experts, position].astype(jnp.float32)
    result = arrived.astype(jnp.float32).at[picks].add(score[:, None] * rows_out)
    return result.astype(jnp.bfloat16)
```

```python
import jax
import jax.numpy as jnp
from jax import lax
from jax.sharding import PartitionSpec as P

D = 8192


EPS = 1e-05


def passed_along(block, axis, distance):
    devices = range(lax.axis_size(axis))
    route = [((i - distance) % len(devices), i) for i in devices]
    return lax.ppermute(block, axis, route)


def feature_product(block, weight):
    return lax.dot_general(
        block, weight, (((1,), (1,)), ((), ())), preferred_element_type=jnp.float32
    )


def slot_map(picks, experts, capacity, slots, tokens):
    count = picks.shape[0]
    order = jnp.arange(count, dtype=jnp.int32)
    earlier = (experts[:, None] == experts[None, :]) & (order[None, :] < order[:, None])
    slot = jnp.sum(earlier.astype(jnp.int32), axis=1)
    target = experts * capacity + slot
    placing = (target[None, :] == jnp.arange(slots, dtype=jnp.int32)[:, None]).astype(jnp.bfloat16)
    picking = (picks[:, None] == jnp.arange(tokens, dtype=jnp.int32)[None, :]).astype(jnp.bfloat16)
    return jnp.dot(placing, picking, preferred_element_type=jnp.float32).astype(jnp.bfloat16)


def body(activations, modality, selected, routes, norm_gain, router, gate_w, up_w, down_w):
    sections, planes = lax.axis_size("section"), lax.axis_size("expert")
    tokens, width = activations.shape
    picks, experts = selected[0], routes[:, 0]
    expert_count = planes * gate_w.shape[0]
    capacity = max(2, 3 * picks.shape[0] // (2 * expert_count))
    slots = expert_count * capacity
    ahead = passed_along(jnp.stack([picks, experts]), "section", -1)
    arrived = passed_along(activations, "section", 1)
    whole = lax.all_gather(
        jnp.concatenate([norm_gain, router[None, :]], axis=0), "expert", axis=1, tiled=True
    )
    place_ahead = slot_map(ahead[0], ahead[1], capacity, slots, tokens)
    place_own = slot_map(picks, experts, capacity, slots, tokens)
    buffer = jnp.dot(place_ahead, activations, preferred_element_type=jnp.float32)
    buffer = buffer.astype(jnp.bfloat16).reshape(planes, capacity, width)
    rows = lax.all_to_all(buffer, "expert", split_axis=0, concat_axis=0, tiled=True)
    rows = rows.transpose(1, 0, 2).reshape(capacity, planes * width).astype(jnp.float32)
    image = lax.axis_index("expert") >= planes // 2
    gain = jnp.where(image, whole[1], whole[0])[None, :]
    scale = lax.rsqrt(jnp.sum(rows * rows, axis=1) / (planes * width) + EPS)
    score = jax.nn.sigmoid(scale * jnp.sum(rows * gain * whole[2][None, :], axis=1))
    normed = (rows * scale[:, None] * gain).astype(jnp.bfloat16)
    scores = lax.all_gather(passed_along(score, "section", 1), "expert", axis=0, tiled=True)
    block = lax.all_gather(normed, "section", axis=0, tiled=True)
    gate = feature_product(block, gate_w[0])
    upper = feature_product(block, up_w[0])
    hidden = (jax.nn.silu(gate) * upper).astype(jnp.bfloat16)
    hidden = jnp.roll(hidden, capacity, axis=0)
    part = jnp.dot(hidden, down_w[0], preferred_element_type=jnp.float32).astype(jnp.bfloat16)
    summed = lax.psum_scatter(part, "section", scatter_dimension=0, tiled=True)
    back = summed.reshape(capacity, planes, width).transpose(1, 0, 2)
    back = lax.all_to_all(back, "expert", split_axis=0, concat_axis=0, tiled=True)
    back = back.reshape(slots, width)
    high = scores.astype(jnp.bfloat16)
    low = (scores - high.astype(jnp.float32)).astype(jnp.bfloat16)
    spread = jnp.concatenate([place_own * high[:, None], place_own * low[:, None]], axis=0)
    added = lax.dot_general(
        spread,
        jnp.concatenate([back, back], axis=0),
        (((0,), (0,)), ((), ())),
        preferred_element_type=jnp.float32,
    )
    return (arrived.astype(jnp.float32) + added).astype(jnp.bfloat16)


def solution(mesh):
    placed = (
        P("section", "expert"),
        P("section"),
        P("section", None),
        P("section", None),
        P(None, "expert"),
        P("expert"),
        P("expert", "section", None),
        P("expert", "section", None),
        P("expert", "section", None),
    )
    return jax.shard_map(
        body, mesh=mesh, in_specs=placed, out_specs=P("section", "expert"), check_vma=False
    )
```

```python
import jax
import jax.numpy as jnp
from jax import lax
from jax.experimental import pallas as pl
from jax.experimental.pallas import tpu as pltpu
from jax.sharding import PartitionSpec as P

D = 8192


EPS = 1e-05


def passed_along(block, axis, distance):
    devices = range(lax.axis_size(axis))
    route = [((i - distance) % len(devices), i) for i in devices]
    return lax.ppermute(block, axis, route)


def feature_product(block, weight):
    return lax.dot_general(
        block, weight, (((1,), (1,)), ((), ())), preferred_element_type=jnp.float32
    )


def slot_map(picks, experts, capacity, slots, tokens):
    count = picks.shape[0]
    order = jnp.arange(count, dtype=jnp.int32)
    earlier = (experts[:, None] == experts[None, :]) & (order[None, :] < order[:, None])
    slot = jnp.sum(earlier.astype(jnp.int32), axis=1)
    target = experts * capacity + slot
    placing = (target[None, :] == jnp.arange(slots, dtype=jnp.int32)[:, None]).astype(jnp.bfloat16)
    picking = (picks[:, None] == jnp.arange(tokens, dtype=jnp.int32)[None, :]).astype(jnp.bfloat16)
    return jnp.dot(placing, picking, preferred_element_type=jnp.float32).astype(jnp.bfloat16)


LANES = 128
MESH = pl.DeviceIdType.MESH


def exchange_kernel(
    rows_in, vectors, gate_hbm, up_hbm, down_hbm, out,
    gate_v, up_v, down_v, came, vec, gathered, gate_sum, up_sum, hidden,
    for_sib, mine, from_sib, relay_x, relay_y, final_x, final_y, done,
    load_sem, z_send, z_recv, vec_send, vec_recv, ag_send, ag_recv, rs_send, rs_recv, back_send, back_recv,
):
    planes, cap, width = rows_in.shape
    full = planes * width
    half = cap // 2
    hid = gate_hbm.shape[0]
    me, plane = lax.axis_index("section"), lax.axis_index("expert")
    core, chip = lax.rem(me, 2), lax.div(me, 2)
    x, y = lax.rem(chip, 2), lax.div(chip, 2)
    sib, xn, yn = me + 1 - 2 * core, me + 2 - 4 * x, me + 4 - 8 * y
    chip_x, chip_y = chip + 1 - 2 * x, chip + 2 - 4 * y
    chip_d = 3 - chip
    dests = {"x": (xn, plane), "y": (yn, plane), "s": (sib, plane)}
    uppers = [lax.rem(plane + j, planes) for j in range(1, planes)]

    barrier = pltpu.get_barrier_semaphore()
    greeted = list(dests.values()) + [(me, p) for p in uppers]
    for device in greeted:
        pl.semaphore_signal(barrier, inc=1, device_id=device, device_id_type=MESH)
    pl.semaphore_wait(barrier, len(greeted))

    sent = []

    def send(src, dst, send_sem, recv_sem, device):
        copy = pltpu.make_async_remote_copy(
            src_ref=src, dst_ref=dst, send_sem=send_sem, recv_sem=recv_sem,
            device_id=device, device_id_type=MESH,
        )
        copy.start()
        sent.append(copy)
        return copy

    z_copies = {}
    vec_copies = [
        send(vectors, vec.at[plane], vec_send.at[j], vec_recv.at[j], (me, p))
        for j, p in enumerate(uppers)
    ]
    for part in range(2):
        piece = pl.ds(part * half, half)
        for j, p in enumerate(uppers):
            n = part * (planes - 1) + j
            z_copies[part, j] = send(
                rows_in.at[p, piece], came.at[plane, piece], z_send.at[n], z_recv.at[n], (me, p)
            )
    local = [
        pltpu.make_async_copy(rows_in.at[plane], came.at[plane], load_sem.at[0]),
        pltpu.make_async_copy(vectors, vec.at[plane], load_sem.at[1]),
        pltpu.make_async_copy(gate_hbm, gate_v, load_sem.at[2]),
        pltpu.make_async_copy(up_hbm, up_v, load_sem.at[3]),
        pltpu.make_async_copy(down_hbm, down_v, load_sem.at[4]),
    ]
    for copy in local:
        copy.start()

    def place(owner_chip, owner_core, part):
        return pl.ds(
            pl.multiple_of((owner_chip * 2 + owner_core) * cap + part * half, 16), half
        )

    image = (plane >= planes // 2).astype(jnp.float32)

    def norm(part):
        @pl.loop(0, half // 16)
        def _(step):
            at = pl.ds(pl.multiple_of(part * half + step * 16, 16), 16)
            to = pl.ds(pl.multiple_of(me * cap + part * half + step * 16, 16), 16)
            squares = jnp.zeros((16, 1), jnp.float32)
            terms = jnp.zeros((16, 1), jnp.float32)
            for q in range(planes):
                rows = came[q, at, :].astype(jnp.float32)
                gain = vec[q, 0:1, :] * (1.0 - image) + vec[q, 1:2, :] * image
                squares += jnp.sum(rows * rows, axis=1, keepdims=True)
                terms += jnp.sum(rows * (gain * vec[q, 2:3, :]), axis=1, keepdims=True)
            scale = lax.rsqrt(squares / full + EPS)
            score = 1.0 / (1.0 + jnp.exp(-(scale * terms)))
            for q in range(planes):
                rows = came[q, at, :].astype(jnp.float32)
                gain = vec[q, 0:1, :] * (1.0 - image) + vec[q, 1:2, :] * image
                gathered[to, q * width : (q + 1) * width] = (rows * scale * gain).astype(jnp.bfloat16)
            high = jnp.broadcast_to(score, (16, LANES)).astype(jnp.bfloat16).astype(jnp.float32)
            lane = lax.broadcasted_iota(jnp.int32, (16, LANES), 1)
            gathered[to, full : full + LANES] = jnp.where(
                lane < LANES // 2, high, score - high
            ).astype(jnp.bfloat16)

    ag = {}
    names = ["x0", "x1", "y0", "y1", "fx", "fy", "s0", "s1", "sx0", "sx1", "sy0", "sy1", "sd0", "sd1"]

    def pass_block(name, owner_chip, part, to):
        ref = gathered.at[place(owner_chip, core, part)]
        n = names.index(name)
        ag[name] = send(ref, ref, ag_send.at[n], ag_recv.at[n], dests[to])

    local[0].wait()
    local[1].wait()
    for copy in vec_copies:
        copy.wait_recv()
    for part in range(2):
        for j in range(planes - 1):
            z_copies[part, j].wait_recv()
        norm(part)
        pass_block(f"x{part}", chip, part, "x")
        pass_block(f"y{part}", chip, part, "y")
        pass_block(f"s{part}", chip, part, "s")

    def products(owner_chip):
        first = pl.multiple_of(owner_chip * 2 * cap, 16)
        gate_sum[...] = jnp.zeros_like(gate_sum)
        up_sum[...] = jnp.zeros_like(up_sum)
        deep = 1024

        @pl.loop(0, full // deep)
        def _(step):
            columns = pl.ds(pl.multiple_of(step * deep, deep), deep)
            block = gathered[pl.ds(first, 2 * cap), columns]
            gate_sum[...] += feature_product(block, gate_v[:, columns])
            up_sum[...] += feature_product(block, up_v[:, columns])

        marks = gathered[pl.ds(first, 2 * cap), full : full + LANES].astype(jnp.float32)
        score = jnp.sum(marks, axis=1, keepdims=True) * (2.0 / LANES)
        gate = gate_sum[...]
        value = gate / (1.0 + jnp.exp(-gate)) * up_sum[...] * score
        value = value.astype(jnp.bfloat16)
        hidden[1, pl.ds(pl.multiple_of(owner_chip * cap, 16), cap), :] = value[:cap]
        after = lax.rem(owner_chip + 1, 4)
        hidden[0, pl.ds(pl.multiple_of(after * cap, 16), cap), :] = value[cap:]

    ag["x0"].wait_recv()
    pass_block("fy", chip_x, 0, "y")
    pass_block("sx0", chip_x, 0, "s")
    ag["y0"].wait_recv()
    pass_block("sy0", chip_y, 0, "s")
    ag["s0"].wait_recv()
    ag["s1"].wait_recv()
    local[2].wait()
    local[3].wait()
    products(chip)
    ag["y1"].wait_recv()
    pass_block("fx", chip_y, 1, "x")
    pass_block("sy1", chip_y, 1, "s")
    ag["x1"].wait_recv()
    pass_block("sx1", chip_x, 1, "s")
    ag["sx0"].wait_recv()
    ag["sx1"].wait_recv()
    products(chip_x)
    ag["fy"].wait_recv()
    pass_block("sd0", chip_d, 0, "s")
    ag["sy0"].wait_recv()
    ag["sy1"].wait_recv()
    products(chip_y)
    ag["fx"].wait_recv()
    pass_block("sd1", chip_d, 1, "s")
    ag["sd0"].wait_recv()
    ag["sd1"].wait_recv()
    products(chip_d)
    local[4].wait()

    rs = {}
    targets = [lax.rem(plane + 1 + i, planes) for i in range(planes)]

    def give(kind, n, i, src, dst, to):
        at = n * planes + i
        rs[kind, i] = send(src, dst, rs_send.at[at], rs_recv.at[at], dests[to])

    def down(i, which, into):
        wide = 512

        @pl.loop(0, width // wide)
        def _(step):
            columns = pl.ds(pl.multiple_of(targets[i] * width + step * wide, wide), wide)
            to = pl.ds(pl.multiple_of(step * wide, wide), wide)
            into[i, :, to] = jnp.dot(
                hidden[which], down_v[:, columns], preferred_element_type=jnp.float32
            ).astype(jnp.bfloat16)

    def start_sums(i):
        down(i, 1 - core, for_sib)
        give("s", 0, i, for_sib.at[i], from_sib.at[i], "s")
        down(i, core, mine)

    def add_into(ref, i, first, count, others):
        @pl.loop(0, count // 16)
        def _(step):
            at = pl.ds(pl.multiple_of(first + step * 16, 16), 16)
            total = mine[i, at, :].astype(jnp.float32)
            for other, begin in others:
                rows = pl.ds(pl.multiple_of(begin + step * 16, 16), 16)
                total += other[i, rows, :].astype(jnp.float32)
            if ref is None:
                mine[i, at, :] = total.astype(jnp.bfloat16)
            else:
                ref[i, pl.ds(pl.multiple_of(step * 16, 16), 16), :] = total.astype(jnp.bfloat16)

    def chip_sums(i):
        rs["s", i].wait_recv()
        for other in (chip_d, chip_x, chip_y):
            base = pl.multiple_of(other * cap, 16)
            add_into(None, i, base, cap, [(from_sib, base)])
            low, high = pl.ds(base, half), pl.ds(pl.multiple_of(base + half, 16), half)
            if other is chip_d:
                give("rx", 1, i, mine.at[i, low], relay_x.at[i], "x")
                give("ry", 2, i, mine.at[i, high], relay_y.at[i], "y")
            elif other is chip_x:
                give("x0", 3, i, mine.at[i, low], final_x.at[i, pl.ds(0, half)], "x")
            else:
                give("y1", 4, i, mine.at[i, high], final_y.at[i, pl.ds(half, half)], "y")

    def relay_sums(i):
        rs["rx", i].wait_recv()
        first = pl.multiple_of(chip_y * cap, 16)
        add_into(None, i, first, half, [(relay_x, 0)])
        give("y0", 5, i, mine.at[i, pl.ds(first, half)], final_y.at[i, pl.ds(0, half)], "y")
        rs["ry", i].wait_recv()
        first = pl.multiple_of(chip_x * cap + half, 16)
        add_into(None, i, first, half, [(relay_y, 0)])
        give("x1", 6, i, mine.at[i, pl.ds(first, half)], final_x.at[i, pl.ds(half, half)], "x")

    back = []

    def final_sums(i):
        for kind in ("x0", "y1", "y0", "x1"):
            rs[kind, i].wait_recv()
        base = pl.multiple_of(chip * cap, 16)
        add_into(done, i, base, cap, [(from_sib, base), (final_x, 0), (final_y, 0)])
        if i < planes - 1:
            back.append(
                send(done.at[i], out.at[plane], back_send.at[i], back_recv.at[i], (me, targets[i]))
            )

    start_sums(0)
    start_sums(1)
    chip_sums(0)
    start_sums(2)
    start_sums(3)
    chip_sums(1)
    relay_sums(0)
    chip_sums(2)
    relay_sums(1)
    final_sums(0)
    chip_sums(3)
    relay_sums(2)
    final_sums(1)
    relay_sums(3)
    final_sums(2)
    final_sums(3)
    own = pltpu.make_async_copy(done.at[planes - 1], out.at[plane], load_sem.at[5])
    own.start()
    for copy in back:
        copy.wait_recv()
    own.wait()
    for copy in sent:
        copy.wait_send()


def exchanged(buffer, vectors, gate, up, down):
    planes, cap, width = buffer.shape
    hid, full = gate.shape
    half, chips = cap // 2, 4
    bf, dma = jnp.bfloat16, pltpu.SemaphoreType.DMA
    anywhere = pl.BlockSpec(memory_space=pl.ANY)
    return pl.pallas_call(
        exchange_kernel,
        out_shape=jax.ShapeDtypeStruct(buffer.shape, bf),
        in_specs=[anywhere] * 5,
        out_specs=anywhere,
        scratch_shapes=[
            pltpu.VMEM((hid, full), bf),
            pltpu.VMEM((hid, full), bf),
            pltpu.VMEM((hid, full), bf),
            pltpu.VMEM((planes, cap, width), bf),
            pltpu.VMEM((planes,) + vectors.shape, jnp.float32),
            pltpu.VMEM((2 * chips * cap, full + LANES), bf),
            pltpu.VMEM((2 * cap, hid), jnp.float32),
            pltpu.VMEM((2 * cap, hid), jnp.float32),
            pltpu.VMEM((2, chips * cap, hid), bf),
            pltpu.VMEM((planes, chips * cap, width), bf),
            pltpu.VMEM((planes, chips * cap, width), bf),
            pltpu.VMEM((planes, chips * cap, width), bf),
            pltpu.VMEM((planes, half, width), bf),
            pltpu.VMEM((planes, half, width), bf),
            pltpu.VMEM((planes, cap, width), bf),
            pltpu.VMEM((planes, cap, width), bf),
            pltpu.VMEM((planes, cap, width), bf),
            dma((6,)),
            dma((2 * (planes - 1),)),
            dma((2 * (planes - 1),)),
            dma((planes - 1,)),
            dma((planes - 1,)),
            dma((14,)),
            dma((14,)),
            dma((7 * planes,)),
            dma((7 * planes,)),
            dma((planes - 1,)),
            dma((planes - 1,)),
        ],
        compiler_params=pltpu.CompilerParams(
            collective_id=0, has_side_effects=True, vmem_limit_bytes=63 * 1024 * 1024
        ),
        cost_estimate=pl.CostEstimate(
            flops=6 * 2 * chips * cap * hid * full, bytes_accessed=6 * hid * full, transcendentals=0
        ),
    )(buffer, vectors, gate, up, down)


def body(activations, modality, selected, routes, norm_gain, router, gate_w, up_w, down_w):
    sections, planes = lax.axis_size("section"), lax.axis_size("expert")
    tokens, width = activations.shape
    picks, experts = selected[0], routes[:, 0]
    expert_count = planes * gate_w.shape[0]
    capacity = max(2, 3 * picks.shape[0] // (2 * expert_count))
    slots = expert_count * capacity
    ahead = passed_along(jnp.stack([picks, experts]), "section", -1)
    arrived = passed_along(activations, "section", 1)
    place_ahead = slot_map(ahead[0], ahead[1], capacity, slots, tokens)
    place_own = slot_map(picks, experts, capacity, slots, tokens)
    buffer = jnp.dot(place_ahead, activations, preferred_element_type=jnp.float32)
    buffer = buffer.astype(jnp.bfloat16).reshape(planes, capacity, width)
    if (sections, planes) == (8, 4) and capacity % 32 == 0:
        vectors = jnp.concatenate(
            [norm_gain, router[None, :], jnp.zeros((5, width), jnp.float32)], axis=0
        )
        back = exchanged(buffer, vectors, gate_w[0], up_w[0], down_w[0]).reshape(slots, width)
        added = lax.dot_general(
            place_own, back, (((0,), (0,)), ((), ())), preferred_element_type=jnp.float32
        )
        return (arrived.astype(jnp.float32) + added).astype(jnp.bfloat16)
    whole = lax.all_gather(
        jnp.concatenate([norm_gain, router[None, :]], axis=0), "expert", axis=1, tiled=True
    )
    rows = lax.all_to_all(buffer, "expert", split_axis=0, concat_axis=0, tiled=True)
    rows = rows.transpose(1, 0, 2).reshape(capacity, planes * width).astype(jnp.float32)
    image = lax.axis_index("expert") >= planes // 2
    gain = jnp.where(image, whole[1], whole[0])[None, :]
    scale = lax.rsqrt(jnp.sum(rows * rows, axis=1) / (planes * width) + EPS)
    score = jax.nn.sigmoid(scale * jnp.sum(rows * gain * whole[2][None, :], axis=1))
    normed = (rows * scale[:, None] * gain).astype(jnp.bfloat16)
    scores = lax.all_gather(passed_along(score, "section", 1), "expert", axis=0, tiled=True)
    block = lax.all_gather(normed, "section", axis=0, tiled=True)
    gate = feature_product(block, gate_w[0])
    upper = feature_product(block, up_w[0])
    hidden = (jax.nn.silu(gate) * upper).astype(jnp.bfloat16)
    hidden = jnp.roll(hidden, capacity, axis=0)
    part = jnp.dot(hidden, down_w[0], preferred_element_type=jnp.float32).astype(jnp.bfloat16)
    summed = lax.psum_scatter(part, "section", scatter_dimension=0, tiled=True)
    back = summed.reshape(capacity, planes, width).transpose(1, 0, 2)
    back = lax.all_to_all(back, "expert", split_axis=0, concat_axis=0, tiled=True)
    back = back.reshape(slots, width)
    high = scores.astype(jnp.bfloat16)
    low = (scores - high.astype(jnp.float32)).astype(jnp.bfloat16)
    spread = jnp.concatenate([place_own * high[:, None], place_own * low[:, None]], axis=0)
    added = lax.dot_general(
        spread,
        jnp.concatenate([back, back], axis=0),
        (((0,), (0,)), ((), ())),
        preferred_element_type=jnp.float32,
    )
    return (arrived.astype(jnp.float32) + added).astype(jnp.bfloat16)


def solution(mesh):
    placed = (
        P("section", "expert"),
        P("section"),
        P("section", None),
        P("section", None),
        P(None, "expert"),
        P("expert"),
        P("expert", "section", None),
        P("expert", "section", None),
        P("expert", "section", None),
    )
    return jax.shard_map(
        body, mesh=mesh, in_specs=placed, out_specs=P("section", "expert"), check_vma=False
    )
```

```python
import jax
import jax.numpy as jnp
from jax import lax
from jax.experimental import pallas as pl
from jax.experimental.pallas import tpu as pltpu
from jax.sharding import PartitionSpec as P

D = 8192


EPS = 1e-05


def passed_along(block, axis, distance):
    devices = range(lax.axis_size(axis))
    route = [((i - distance) % len(devices), i) for i in devices]
    return lax.ppermute(block, axis, route)


def feature_product(block, weight):
    return lax.dot_general(
        block, weight, (((1,), (1,)), ((), ())), preferred_element_type=jnp.float32
    )


def slot_map(picks, experts, capacity, slots, tokens):
    count = picks.shape[0]
    order = jnp.arange(count, dtype=jnp.int32)
    earlier = (experts[:, None] == experts[None, :]) & (order[None, :] < order[:, None])
    slot = jnp.sum(earlier.astype(jnp.int32), axis=1)
    target = experts * capacity + slot
    placing = (target[None, :] == jnp.arange(slots, dtype=jnp.int32)[:, None]).astype(jnp.bfloat16)
    picking = (picks[:, None] == jnp.arange(tokens, dtype=jnp.int32)[None, :]).astype(jnp.bfloat16)
    return jnp.dot(placing, picking, preferred_element_type=jnp.float32).astype(jnp.bfloat16)


LANES = 128
MESH = pl.DeviceIdType.MESH


def exchange_kernel(
    rows_in, vectors, gate_hbm, up_hbm, down_hbm, out,
    gate_v, up_v, down_v, came, vec, gathered, gate_sum, up_sum, hidden,
    for_sib, mine, from_sib, relay_x, relay_y, final_x, final_y, done,
    load_sem, z_send, z_recv, vec_send, vec_recv, ag_send, ag_recv, rs_send, rs_recv, back_send, back_recv,
):
    planes, cap, width = rows_in.shape
    full = planes * width
    half = cap // 2
    hid = gate_hbm.shape[0]
    me, plane = lax.axis_index("section"), lax.axis_index("expert")
    core, chip = lax.rem(me, 2), lax.div(me, 2)
    x, y = lax.rem(chip, 2), lax.div(chip, 2)
    sib, xn, yn = me + 1 - 2 * core, me + 2 - 4 * x, me + 4 - 8 * y
    chip_x, chip_y = chip + 1 - 2 * x, chip + 2 - 4 * y
    chip_d = 3 - chip
    dests = {"x": (xn, plane), "y": (yn, plane), "s": (sib, plane)}
    uppers = [lax.rem(plane + j, planes) for j in range(1, planes)]

    barrier = pltpu.get_barrier_semaphore()
    greeted = list(dests.values()) + [(me, p) for p in uppers]
    for device in greeted:
        pl.semaphore_signal(barrier, inc=1, device_id=device, device_id_type=MESH)
    pl.semaphore_wait(barrier, len(greeted))

    sent = []

    def send(src, dst, send_sem, recv_sem, device):
        copy = pltpu.make_async_remote_copy(
            src_ref=src, dst_ref=dst, send_sem=send_sem, recv_sem=recv_sem,
            device_id=device, device_id_type=MESH,
        )
        copy.start()
        sent.append(copy)
        return copy

    z_copies = {}
    vec_copies = [
        send(vectors, vec.at[plane], vec_send.at[j], vec_recv.at[j], (me, p))
        for j, p in enumerate(uppers)
    ]
    for part in range(2):
        piece = pl.ds(part * half, half)
        for j, p in enumerate(uppers):
            n = part * (planes - 1) + j
            z_copies[part, j] = send(
                rows_in.at[p, piece], came.at[plane, piece], z_send.at[n], z_recv.at[n], (me, p)
            )
    local = [
        pltpu.make_async_copy(rows_in.at[plane], came.at[plane], load_sem.at[0]),
        pltpu.make_async_copy(vectors, vec.at[plane], load_sem.at[1]),
        pltpu.make_async_copy(gate_hbm, gate_v, load_sem.at[2]),
        pltpu.make_async_copy(up_hbm, up_v, load_sem.at[3]),
        pltpu.make_async_copy(down_hbm, down_v, load_sem.at[4]),
    ]
    for copy in local:
        copy.start()

    def place(owner_chip, owner_core, part):
        return pl.ds(
            pl.multiple_of((owner_chip * 2 + owner_core) * cap + part * half, 16), half
        )

    image = (plane >= planes // 2).astype(jnp.float32)

    def norm(part):
        @pl.loop(0, half // 16)
        def _(step):
            at = pl.ds(pl.multiple_of(part * half + step * 16, 16), 16)
            to = pl.ds(pl.multiple_of(me * cap + part * half + step * 16, 16), 16)
            squares = jnp.zeros((16, 1), jnp.float32)
            terms = jnp.zeros((16, 1), jnp.float32)
            for q in range(planes):
                rows = came[q, at, :].astype(jnp.float32)
                gain = vec[q, 0:1, :] * (1.0 - image) + vec[q, 1:2, :] * image
                squares += jnp.sum(rows * rows, axis=1, keepdims=True)
                terms += jnp.sum(rows * (gain * vec[q, 2:3, :]), axis=1, keepdims=True)
            scale = lax.rsqrt(squares / full + EPS)
            score = 1.0 / (1.0 + jnp.exp(-(scale * terms)))
            for q in range(planes):
                rows = came[q, at, :].astype(jnp.float32)
                gain = vec[q, 0:1, :] * (1.0 - image) + vec[q, 1:2, :] * image
                gathered[to, q * width : (q + 1) * width] = (rows * scale * gain).astype(jnp.bfloat16)
            high = jnp.broadcast_to(score, (16, LANES)).astype(jnp.bfloat16).astype(jnp.float32)
            lane = lax.broadcasted_iota(jnp.int32, (16, LANES), 1)
            gathered[to, full : full + LANES] = jnp.where(
                lane < LANES // 2, high, score - high
            ).astype(jnp.bfloat16)

    ag = {}
    names = ["x0", "x1", "y0", "y1", "fx", "fy", "s0", "s1", "sx0", "sx1", "sy0", "sy1", "sd0", "sd1"]

    def pass_block(name, owner_chip, part, to):
        ref = gathered.at[place(owner_chip, core, part)]
        n = names.index(name)
        ag[name] = send(ref, ref, ag_send.at[n], ag_recv.at[n], dests[to])

    local[0].wait()
    local[1].wait()
    for copy in vec_copies:
        copy.wait_recv()
    for part in range(2):
        for j in range(planes - 1):
            z_copies[part, j].wait_recv()
        norm(part)
        pass_block(f"x{part}", chip, part, "x")
        pass_block(f"y{part}", chip, part, "y")
        pass_block(f"s{part}", chip, part, "s")

    def products(owner_chip):
        first = pl.multiple_of(owner_chip * 2 * cap, 16)
        gate_sum[...] = jnp.zeros_like(gate_sum)
        up_sum[...] = jnp.zeros_like(up_sum)
        deep = 1024

        @pl.loop(0, full // deep)
        def _(step):
            columns = pl.ds(pl.multiple_of(step * deep, deep), deep)
            block = gathered[pl.ds(first, 2 * cap), columns]
            gate_sum[...] += feature_product(gate_v[:, columns], block)
            up_sum[...] += feature_product(up_v[:, columns], block)

        marks = gathered[pl.ds(first, 2 * cap), full : full + LANES].astype(jnp.float32)
        score = jnp.sum(marks, axis=1, keepdims=True) * (2.0 / LANES)
        gate = gate_sum[...]
        value = gate / (1.0 + jnp.exp(-gate)) * up_sum[...]
        value = (value.T * score).astype(jnp.bfloat16)
        hidden[1, pl.ds(pl.multiple_of(owner_chip * cap, 16), cap), :] = value[:cap]
        after = lax.rem(owner_chip + 1, 4)
        hidden[0, pl.ds(pl.multiple_of(after * cap, 16), cap), :] = value[cap:]

    ag["x0"].wait_recv()
    pass_block("fy", chip_x, 0, "y")
    pass_block("sx0", chip_x, 0, "s")
    ag["y0"].wait_recv()
    pass_block("sy0", chip_y, 0, "s")
    ag["s0"].wait_recv()
    ag["s1"].wait_recv()
    local[2].wait()
    local[3].wait()
    products(chip)
    ag["y1"].wait_recv()
    pass_block("fx", chip_y, 1, "x")
    pass_block("sy1", chip_y, 1, "s")
    ag["x1"].wait_recv()
    pass_block("sx1", chip_x, 1, "s")
    ag["sx0"].wait_recv()
    ag["sx1"].wait_recv()
    products(chip_x)
    ag["fy"].wait_recv()
    pass_block("sd0", chip_d, 0, "s")
    ag["sy0"].wait_recv()
    ag["sy1"].wait_recv()
    products(chip_y)
    ag["fx"].wait_recv()
    pass_block("sd1", chip_d, 1, "s")
    ag["sd0"].wait_recv()
    ag["sd1"].wait_recv()
    products(chip_d)
    local[4].wait()

    rs = {}
    targets = [lax.rem(plane + 1 + i, planes) for i in range(planes)]

    def give(kind, n, i, src, dst, to):
        at = n * planes + i
        rs[kind, i] = send(src, dst, rs_send.at[at], rs_recv.at[at], dests[to])

    def down(i, which, into):
        wide = 512

        @pl.loop(0, width // wide)
        def _(step):
            columns = pl.ds(pl.multiple_of(targets[i] * width + step * wide, wide), wide)
            to = pl.ds(pl.multiple_of(step * wide, wide), wide)
            into[i, :, to] = jnp.dot(
                hidden[which], down_v[:, columns], preferred_element_type=jnp.float32
            ).astype(jnp.bfloat16)

    def start_sums(i):
        down(i, 1 - core, for_sib)
        give("s", 0, i, for_sib.at[i], from_sib.at[i], "s")
        down(i, core, mine)

    def add_into(ref, i, first, count, others):
        @pl.loop(0, count // 16)
        def _(step):
            at = pl.ds(pl.multiple_of(first + step * 16, 16), 16)
            total = mine[i, at, :].astype(jnp.float32)
            for other, begin in others:
                rows = pl.ds(pl.multiple_of(begin + step * 16, 16), 16)
                total += other[i, rows, :].astype(jnp.float32)
            if ref is None:
                mine[i, at, :] = total.astype(jnp.bfloat16)
            else:
                ref[i, pl.ds(pl.multiple_of(step * 16, 16), 16), :] = total.astype(jnp.bfloat16)

    def chip_sums(i):
        rs["s", i].wait_recv()
        for other in (chip_d, chip_x, chip_y):
            base = pl.multiple_of(other * cap, 16)
            add_into(None, i, base, cap, [(from_sib, base)])
            low, high = pl.ds(base, half), pl.ds(pl.multiple_of(base + half, 16), half)
            if other is chip_d:
                give("rx", 1, i, mine.at[i, low], relay_x.at[i], "x")
                give("ry", 2, i, mine.at[i, high], relay_y.at[i], "y")
            elif other is chip_x:
                give("x0", 3, i, mine.at[i, low], final_x.at[i, pl.ds(0, half)], "x")
            else:
                give("y1", 4, i, mine.at[i, high], final_y.at[i, pl.ds(half, half)], "y")

    def relay_sums(i):
        rs["rx", i].wait_recv()
        first = pl.multiple_of(chip_y * cap, 16)
        add_into(None, i, first, half, [(relay_x, 0)])
        give("y0", 5, i, mine.at[i, pl.ds(first, half)], final_y.at[i, pl.ds(0, half)], "y")
        rs["ry", i].wait_recv()
        first = pl.multiple_of(chip_x * cap + half, 16)
        add_into(None, i, first, half, [(relay_y, 0)])
        give("x1", 6, i, mine.at[i, pl.ds(first, half)], final_x.at[i, pl.ds(half, half)], "x")

    back = []

    def final_sums(i):
        for kind in ("x0", "y1", "y0", "x1"):
            rs[kind, i].wait_recv()
        base = pl.multiple_of(chip * cap, 16)
        add_into(done, i, base, cap, [(from_sib, base), (final_x, 0), (final_y, 0)])
        if i < planes - 1:
            back.append(
                send(done.at[i], out.at[plane], back_send.at[i], back_recv.at[i], (me, targets[i]))
            )

    start_sums(0)
    start_sums(1)
    chip_sums(0)
    start_sums(2)
    start_sums(3)
    chip_sums(1)
    relay_sums(0)
    chip_sums(2)
    relay_sums(1)
    final_sums(0)
    chip_sums(3)
    relay_sums(2)
    final_sums(1)
    relay_sums(3)
    final_sums(2)
    final_sums(3)
    own = pltpu.make_async_copy(done.at[planes - 1], out.at[plane], load_sem.at[5])
    own.start()
    for copy in back:
        copy.wait_recv()
    own.wait()
    for copy in sent:
        copy.wait_send()


def exchanged(buffer, vectors, gate, up, down):
    planes, cap, width = buffer.shape
    hid, full = gate.shape
    half, chips = cap // 2, 4
    bf, dma = jnp.bfloat16, pltpu.SemaphoreType.DMA
    anywhere = pl.BlockSpec(memory_space=pl.ANY)
    return pl.pallas_call(
        exchange_kernel,
        out_shape=jax.ShapeDtypeStruct(buffer.shape, bf),
        in_specs=[anywhere] * 5,
        out_specs=anywhere,
        scratch_shapes=[
            pltpu.VMEM((hid, full), bf),
            pltpu.VMEM((hid, full), bf),
            pltpu.VMEM((hid, full), bf),
            pltpu.VMEM((planes, cap, width), bf),
            pltpu.VMEM((planes,) + vectors.shape, jnp.float32),
            pltpu.VMEM((2 * chips * cap, full + LANES), bf),
            pltpu.VMEM((hid, 2 * cap), jnp.float32),
            pltpu.VMEM((hid, 2 * cap), jnp.float32),
            pltpu.VMEM((2, chips * cap, hid), bf),
            pltpu.VMEM((planes, chips * cap, width), bf),
            pltpu.VMEM((planes, chips * cap, width), bf),
            pltpu.VMEM((planes, chips * cap, width), bf),
            pltpu.VMEM((planes, half, width), bf),
            pltpu.VMEM((planes, half, width), bf),
            pltpu.VMEM((planes, cap, width), bf),
            pltpu.VMEM((planes, cap, width), bf),
            pltpu.VMEM((planes, cap, width), bf),
            dma((6,)),
            dma((2 * (planes - 1),)),
            dma((2 * (planes - 1),)),
            dma((planes - 1,)),
            dma((planes - 1,)),
            dma((14,)),
            dma((14,)),
            dma((7 * planes,)),
            dma((7 * planes,)),
            dma((planes - 1,)),
            dma((planes - 1,)),
        ],
        compiler_params=pltpu.CompilerParams(
            collective_id=0, has_side_effects=True, vmem_limit_bytes=63 * 1024 * 1024
        ),
        cost_estimate=pl.CostEstimate(
            flops=6 * 2 * chips * cap * hid * full, bytes_accessed=6 * hid * full, transcendentals=0
        ),
    )(buffer, vectors, gate, up, down)


def body(activations, modality, selected, routes, norm_gain, router, gate_w, up_w, down_w):
    sections, planes = lax.axis_size("section"), lax.axis_size("expert")
    tokens, width = activations.shape
    picks, experts = selected[0], routes[:, 0]
    expert_count = planes * gate_w.shape[0]
    capacity = max(2, 3 * picks.shape[0] // (2 * expert_count))
    slots = expert_count * capacity
    ahead = passed_along(jnp.stack([picks, experts]), "section", -1)
    arrived = passed_along(activations, "section", 1)
    place_own = lax.optimization_barrier(slot_map(picks, experts, capacity, slots, tokens))
    place_ahead = lax.optimization_barrier(
        slot_map(ahead[0], ahead[1], capacity, slots, tokens)
    )
    buffer = jnp.dot(place_ahead, activations, preferred_element_type=jnp.float32)
    buffer = buffer.astype(jnp.bfloat16).reshape(planes, capacity, width)
    if (sections, planes) == (8, 4) and capacity % 32 == 0:
        vectors = jnp.concatenate(
            [norm_gain, router[None, :], jnp.zeros((5, width), jnp.float32)], axis=0
        )
        back = exchanged(buffer, vectors, gate_w[0], up_w[0], down_w[0]).reshape(slots, width)
        added = lax.dot_general(
            place_own, back, (((0,), (0,)), ((), ())), preferred_element_type=jnp.float32
        )
        return (arrived.astype(jnp.float32) + added).astype(jnp.bfloat16)
    whole = lax.all_gather(
        jnp.concatenate([norm_gain, router[None, :]], axis=0), "expert", axis=1, tiled=True
    )
    rows = lax.all_to_all(buffer, "expert", split_axis=0, concat_axis=0, tiled=True)
    rows = rows.transpose(1, 0, 2).reshape(capacity, planes * width).astype(jnp.float32)
    image = lax.axis_index("expert") >= planes // 2
    gain = jnp.where(image, whole[1], whole[0])[None, :]
    scale = lax.rsqrt(jnp.sum(rows * rows, axis=1) / (planes * width) + EPS)
    score = jax.nn.sigmoid(scale * jnp.sum(rows * gain * whole[2][None, :], axis=1))
    normed = (rows * scale[:, None] * gain).astype(jnp.bfloat16)
    scores = lax.all_gather(passed_along(score, "section", 1), "expert", axis=0, tiled=True)
    block = lax.all_gather(normed, "section", axis=0, tiled=True)
    gate = feature_product(block, gate_w[0])
    upper = feature_product(block, up_w[0])
    hidden = (jax.nn.silu(gate) * upper).astype(jnp.bfloat16)
    hidden = jnp.roll(hidden, capacity, axis=0)
    part = jnp.dot(hidden, down_w[0], preferred_element_type=jnp.float32).astype(jnp.bfloat16)
    summed = lax.psum_scatter(part, "section", scatter_dimension=0, tiled=True)
    back = summed.reshape(capacity, planes, width).transpose(1, 0, 2)
    back = lax.all_to_all(back, "expert", split_axis=0, concat_axis=0, tiled=True)
    back = back.reshape(slots, width)
    high = scores.astype(jnp.bfloat16)
    low = (scores - high.astype(jnp.float32)).astype(jnp.bfloat16)
    spread = jnp.concatenate([place_own * high[:, None], place_own * low[:, None]], axis=0)
    added = lax.dot_general(
        spread,
        jnp.concatenate([back, back], axis=0),
        (((0,), (0,)), ((), ())),
        preferred_element_type=jnp.float32,
    )
    return (arrived.astype(jnp.float32) + added).astype(jnp.bfloat16)


def solution(mesh):
    placed = (
        P("section", "expert"),
        P("section"),
        P("section", None),
        P("section", None),
        P(None, "expert"),
        P("expert"),
        P("expert", "section", None),
        P("expert", "section", None),
        P("expert", "section", None),
    )
    return jax.shard_map(
        body, mesh=mesh, in_specs=placed, out_specs=P("section", "expert"), check_vma=False
    )
```

```python
import jax
import jax.numpy as jnp
from jax import lax
from jax.experimental import pallas as pl
from jax.experimental.pallas import tpu as pltpu
from jax.sharding import PartitionSpec as P

D = 8192


EPS = 1e-05


def passed_along(block, axis, distance):
    devices = range(lax.axis_size(axis))
    route = [((i - distance) % len(devices), i) for i in devices]
    return lax.ppermute(block, axis, route)


def feature_product(block, weight):
    return lax.dot_general(
        block, weight, (((1,), (1,)), ((), ())), preferred_element_type=jnp.float32
    )


def slot_map(picks, experts, capacity, slots, tokens):
    count = picks.shape[0]
    order = jnp.arange(count, dtype=jnp.int32)
    earlier = (experts[:, None] == experts[None, :]) & (order[None, :] < order[:, None])
    slot = jnp.sum(earlier.astype(jnp.int32), axis=1)
    target = experts * capacity + slot
    placing = (target[None, :] == jnp.arange(slots, dtype=jnp.int32)[:, None]).astype(jnp.bfloat16)
    picking = (picks[:, None] == jnp.arange(tokens, dtype=jnp.int32)[None, :]).astype(jnp.bfloat16)
    return jnp.dot(placing, picking, preferred_element_type=jnp.float32).astype(jnp.bfloat16)


LANES = 128
MESH = pl.DeviceIdType.MESH


def exchange_kernel(
    rows_in, vectors, gate_hbm, up_hbm, down_hbm, leaving, out, arrived,
    gate_v, up_v, down_v, came, vec, gathered, gate_sum, up_sum, hidden,
    for_sib, mine, from_sib, relay_x, relay_y, final_x, final_y, done,
    load_sem, z_send, z_recv, vec_send, vec_recv, ag_send, ag_recv, rs_send, rs_recv, back_send, back_recv,
    shift_send, shift_recv,
):
    planes, cap, width = rows_in.shape
    full = planes * width
    half = cap // 2
    hid = gate_hbm.shape[0]
    me, plane = lax.axis_index("section"), lax.axis_index("expert")
    core, chip = lax.rem(me, 2), lax.div(me, 2)
    x, y = lax.rem(chip, 2), lax.div(chip, 2)
    sib, xn, yn = me + 1 - 2 * core, me + 2 - 4 * x, me + 4 - 8 * y
    chip_x, chip_y = chip + 1 - 2 * x, chip + 2 - 4 * y
    chip_d = 3 - chip
    dests = {"x": (xn, plane), "y": (yn, plane), "s": (sib, plane)}
    uppers = [lax.rem(plane + j, planes) for j in range(1, planes)]

    sections = lax.axis_size("section")
    following, previous = lax.rem(me + 1, sections), lax.rem(me + sections - 1, sections)

    barrier = pltpu.get_barrier_semaphore()
    greeted = list(dests.values()) + [(me, p) for p in uppers]
    greeted += [(following, plane), (previous, plane)]
    for device in greeted:
        pl.semaphore_signal(barrier, inc=1, device_id=device, device_id_type=MESH)
    pl.semaphore_wait(barrier, len(greeted))

    sent = []

    def send(src, dst, send_sem, recv_sem, device):
        copy = pltpu.make_async_remote_copy(
            src_ref=src, dst_ref=dst, send_sem=send_sem, recv_sem=recv_sem,
            device_id=device, device_id_type=MESH,
        )
        copy.start()
        sent.append(copy)
        return copy

    early = leaving.shape[0] * 5 // 8
    parts = [pl.ds(0, early), pl.ds(early, leaving.shape[0] - early)]

    def shift(n):
        return send(
            leaving.at[parts[n]], arrived.at[parts[n]],
            shift_send.at[n], shift_recv.at[n], (following, plane),
        )

    z_copies = {}
    vec_copies = [
        send(vectors, vec.at[plane], vec_send.at[j], vec_recv.at[j], (me, p))
        for j, p in enumerate(uppers)
    ]

    def to_planes(part):
        piece = pl.ds(part * half, half)
        for j, p in enumerate(uppers):
            n = part * (planes - 1) + j
            z_copies[part, j] = send(
                rows_in.at[p, piece], came.at[plane, piece], z_send.at[n], z_recv.at[n], (me, p)
            )

    to_planes(0)
    shifts = [shift(0)]
    local = [
        pltpu.make_async_copy(rows_in.at[plane], came.at[plane], load_sem.at[0]),
        pltpu.make_async_copy(vectors, vec.at[plane], load_sem.at[1]),
        pltpu.make_async_copy(gate_hbm, gate_v, load_sem.at[2]),
        pltpu.make_async_copy(up_hbm, up_v, load_sem.at[3]),
        pltpu.make_async_copy(down_hbm, down_v, load_sem.at[4]),
    ]
    for copy in local:
        copy.start()
    for j in range(planes - 1):
        z_copies[0, j].wait_send()
    sent[:] = [copy for copy in sent if all(copy is not z_copies[0, j] for j in range(planes - 1))]
    to_planes(1)

    def place(owner_chip, owner_core, part):
        return pl.ds(
            pl.multiple_of((owner_chip * 2 + owner_core) * cap + part * half, 16), half
        )

    image = (plane >= planes // 2).astype(jnp.float32)

    def norm(part):
        @pl.loop(0, half // 16)
        def _(step):
            at = pl.ds(pl.multiple_of(part * half + step * 16, 16), 16)
            to = pl.ds(pl.multiple_of(me * cap + part * half + step * 16, 16), 16)
            squares = jnp.zeros((16, 1), jnp.float32)
            terms = jnp.zeros((16, 1), jnp.float32)
            for q in range(planes):
                rows = came[q, at, :].astype(jnp.float32)
                gain = vec[q, 0:1, :] * (1.0 - image) + vec[q, 1:2, :] * image
                squares += jnp.sum(rows * rows, axis=1, keepdims=True)
                terms += jnp.sum(rows * (gain * vec[q, 2:3, :]), axis=1, keepdims=True)
            scale = lax.rsqrt(squares / full + EPS)
            score = 1.0 / (1.0 + jnp.exp(-(scale * terms)))
            for q in range(planes):
                rows = came[q, at, :].astype(jnp.float32)
                gain = vec[q, 0:1, :] * (1.0 - image) + vec[q, 1:2, :] * image
                gathered[to, q * width : (q + 1) * width] = (rows * scale * gain).astype(jnp.bfloat16)
            high = jnp.broadcast_to(score, (16, LANES)).astype(jnp.bfloat16).astype(jnp.float32)
            lane = lax.broadcasted_iota(jnp.int32, (16, LANES), 1)
            gathered[to, full : full + LANES] = jnp.where(
                lane < LANES // 2, high, score - high
            ).astype(jnp.bfloat16)

    ag = {}
    names = ["x0", "x1", "y0", "y1", "fx", "fy", "s0", "s1", "sx0", "sx1", "sy0", "sy1", "sd0", "sd1"]

    def pass_block(name, owner_chip, part, to):
        ref = gathered.at[place(owner_chip, core, part)]
        n = names.index(name)
        ag[name] = send(ref, ref, ag_send.at[n], ag_recv.at[n], dests[to])

    local[0].wait()
    local[1].wait()
    for copy in vec_copies:
        copy.wait_recv()
    for part in range(2):
        for j in range(planes - 1):
            z_copies[part, j].wait_recv()
        norm(part)
        pass_block(f"x{part}", chip, part, "x")
        pass_block(f"y{part}", chip, part, "y")
        pass_block(f"s{part}", chip, part, "s")

    def products(owner_chip):
        first = pl.multiple_of(owner_chip * 2 * cap, 16)
        gate_sum[...] = jnp.zeros_like(gate_sum)
        up_sum[...] = jnp.zeros_like(up_sum)
        deep = 1024

        @pl.loop(0, full // deep)
        def _(step):
            columns = pl.ds(pl.multiple_of(step * deep, deep), deep)
            block = gathered[pl.ds(first, 2 * cap), columns]
            gate_sum[...] += feature_product(gate_v[:, columns], block)
            up_sum[...] += feature_product(up_v[:, columns], block)

        marks = gathered[pl.ds(first, 2 * cap), full : full + LANES].astype(jnp.float32)
        score = jnp.sum(marks, axis=1, keepdims=True) * (2.0 / LANES)
        gate = gate_sum[...]
        value = gate / (1.0 + jnp.exp(-gate)) * up_sum[...]
        value = (value.T * score).astype(jnp.bfloat16)
        hidden[1, pl.ds(pl.multiple_of(owner_chip * cap, 16), cap), :] = value[:cap]
        after = lax.rem(owner_chip + 1, 4)
        hidden[0, pl.ds(pl.multiple_of(after * cap, 16), cap), :] = value[cap:]

    ag["x0"].wait_recv()
    pass_block("fy", chip_x, 0, "y")
    pass_block("sx0", chip_x, 0, "s")
    ag["y0"].wait_recv()
    pass_block("sy0", chip_y, 0, "s")
    ag["s0"].wait_recv()
    ag["s1"].wait_recv()
    local[2].wait()
    local[3].wait()
    products(chip)
    ag["y1"].wait_recv()
    pass_block("fx", chip_y, 1, "x")
    pass_block("sy1", chip_y, 1, "s")
    ag["x1"].wait_recv()
    pass_block("sx1", chip_x, 1, "s")
    ag["sx0"].wait_recv()
    ag["sx1"].wait_recv()
    products(chip_x)
    ag["fy"].wait_recv()
    pass_block("sd0", chip_d, 0, "s")
    ag["sy0"].wait_recv()
    ag["sy1"].wait_recv()
    products(chip_y)
    ag["fx"].wait_recv()
    pass_block("sd1", chip_d, 1, "s")
    shifts.append(shift(1))
    ag["sd0"].wait_recv()
    ag["sd1"].wait_recv()
    products(chip_d)
    local[4].wait()

    rs = {}
    targets = [lax.rem(plane + 1 + i, planes) for i in range(planes)]

    def give(kind, n, i, src, dst, to):
        at = n * planes + i
        rs[kind, i] = send(src, dst, rs_send.at[at], rs_recv.at[at], dests[to])

    def down(i, which, into):
        wide = 512

        @pl.loop(0, width // wide)
        def _(step):
            columns = pl.ds(pl.multiple_of(targets[i] * width + step * wide, wide), wide)
            to = pl.ds(pl.multiple_of(step * wide, wide), wide)
            into[i, :, to] = jnp.dot(
                hidden[which], down_v[:, columns], preferred_element_type=jnp.float32
            ).astype(jnp.bfloat16)

    def start_sums(i):
        down(i, 1 - core, for_sib)
        give("s", 0, i, for_sib.at[i], from_sib.at[i], "s")
        down(i, core, mine)

    def add_into(ref, i, first, count, others):
        @pl.loop(0, count // 16)
        def _(step):
            at = pl.ds(pl.multiple_of(first + step * 16, 16), 16)
            total = mine[i, at, :].astype(jnp.float32)
            for other, begin in others:
                rows = pl.ds(pl.multiple_of(begin + step * 16, 16), 16)
                total += other[i, rows, :].astype(jnp.float32)
            if ref is None:
                mine[i, at, :] = total.astype(jnp.bfloat16)
            else:
                ref[i, pl.ds(pl.multiple_of(step * 16, 16), 16), :] = total.astype(jnp.bfloat16)

    def chip_sums(i):
        rs["s", i].wait_recv()
        for other in (chip_d, chip_x, chip_y):
            base = pl.multiple_of(other * cap, 16)
            add_into(None, i, base, cap, [(from_sib, base)])
            low, high = pl.ds(base, half), pl.ds(pl.multiple_of(base + half, 16), half)
            if other is chip_d:
                give("rx", 1, i, mine.at[i, low], relay_x.at[i], "x")
                give("ry", 2, i, mine.at[i, high], relay_y.at[i], "y")
            elif other is chip_x:
                give("x0", 3, i, mine.at[i, low], final_x.at[i, pl.ds(0, half)], "x")
            else:
                give("y1", 4, i, mine.at[i, high], final_y.at[i, pl.ds(half, half)], "y")

    def relay_sums(i):
        rs["rx", i].wait_recv()
        first = pl.multiple_of(chip_y * cap, 16)
        add_into(None, i, first, half, [(relay_x, 0)])
        give("y0", 5, i, mine.at[i, pl.ds(first, half)], final_y.at[i, pl.ds(0, half)], "y")
        rs["ry", i].wait_recv()
        first = pl.multiple_of(chip_x * cap + half, 16)
        add_into(None, i, first, half, [(relay_y, 0)])
        give("x1", 6, i, mine.at[i, pl.ds(first, half)], final_x.at[i, pl.ds(half, half)], "x")

    back = []

    def final_sums(i):
        for kind in ("x0", "y1", "y0", "x1"):
            rs[kind, i].wait_recv()
        base = pl.multiple_of(chip * cap, 16)
        add_into(done, i, base, cap, [(from_sib, base), (final_x, 0), (final_y, 0)])
        if i < planes - 1:
            back.append(
                send(done.at[i], out.at[plane], back_send.at[i], back_recv.at[i], (me, targets[i]))
            )

    start_sums(0)
    start_sums(1)
    chip_sums(0)
    start_sums(2)
    start_sums(3)
    chip_sums(1)
    relay_sums(0)
    chip_sums(2)
    relay_sums(1)
    final_sums(0)
    chip_sums(3)
    relay_sums(2)
    final_sums(1)
    relay_sums(3)
    final_sums(2)
    final_sums(3)
    own = pltpu.make_async_copy(done.at[planes - 1], out.at[plane], load_sem.at[5])
    own.start()
    for copy in back:
        copy.wait_recv()
    own.wait()
    for copy in shifts:
        copy.wait_recv()
    for copy in sent:
        copy.wait_send()


def exchanged(buffer, vectors, gate, up, down, leaving):
    planes, cap, width = buffer.shape
    hid, full = gate.shape
    half, chips = cap // 2, 4
    bf, dma = jnp.bfloat16, pltpu.SemaphoreType.DMA
    anywhere = pl.BlockSpec(memory_space=pl.ANY)
    return pl.pallas_call(
        exchange_kernel,
        out_shape=[
            jax.ShapeDtypeStruct(buffer.shape, bf),
            jax.ShapeDtypeStruct(leaving.shape, bf),
        ],
        in_specs=[anywhere] * 6,
        out_specs=[anywhere] * 2,
        scratch_shapes=[
            pltpu.VMEM((hid, full), bf),
            pltpu.VMEM((hid, full), bf),
            pltpu.VMEM((hid, full), bf),
            pltpu.VMEM((planes, cap, width), bf),
            pltpu.VMEM((planes,) + vectors.shape, jnp.float32),
            pltpu.VMEM((2 * chips * cap, full + LANES), bf),
            pltpu.VMEM((hid, 2 * cap), jnp.float32),
            pltpu.VMEM((hid, 2 * cap), jnp.float32),
            pltpu.VMEM((2, chips * cap, hid), bf),
            pltpu.VMEM((planes, chips * cap, width), bf),
            pltpu.VMEM((planes, chips * cap, width), bf),
            pltpu.VMEM((planes, chips * cap, width), bf),
            pltpu.VMEM((planes, half, width), bf),
            pltpu.VMEM((planes, half, width), bf),
            pltpu.VMEM((planes, cap, width), bf),
            pltpu.VMEM((planes, cap, width), bf),
            pltpu.VMEM((planes, cap, width), bf),
            dma((6,)),
            dma((2 * (planes - 1),)),
            dma((2 * (planes - 1),)),
            dma((planes - 1,)),
            dma((planes - 1,)),
            dma((14,)),
            dma((14,)),
            dma((7 * planes,)),
            dma((7 * planes,)),
            dma((planes - 1,)),
            dma((planes - 1,)),
            dma((2,)),
            dma((2,)),
        ],
        compiler_params=pltpu.CompilerParams(
            collective_id=0, has_side_effects=True, vmem_limit_bytes=63 * 1024 * 1024
        ),
        cost_estimate=pl.CostEstimate(
            flops=6 * 2 * chips * cap * hid * full, bytes_accessed=6 * hid * full, transcendentals=0
        ),
    )(buffer, vectors, gate, up, down, leaving)


def body(activations, modality, selected, routes, norm_gain, router, gate_w, up_w, down_w):
    sections, planes = lax.axis_size("section"), lax.axis_size("expert")
    tokens, width = activations.shape
    picks, experts = selected[0], routes[:, 0]
    expert_count = planes * gate_w.shape[0]
    capacity = max(2, 3 * picks.shape[0] // (2 * expert_count))
    slots = expert_count * capacity
    ahead = passed_along(jnp.stack([picks, experts]), "section", -1)
    place_own = lax.optimization_barrier(slot_map(picks, experts, capacity, slots, tokens))
    place_ahead = lax.optimization_barrier(
        slot_map(ahead[0], ahead[1], capacity, slots, tokens)
    )
    buffer = jnp.dot(place_ahead, activations, preferred_element_type=jnp.float32)
    buffer = buffer.astype(jnp.bfloat16).reshape(planes, capacity, width)
    if (sections, planes) == (8, 4) and capacity % 32 == 0:
        vectors = jnp.concatenate(
            [norm_gain, router[None, :], jnp.zeros((5, width), jnp.float32)], axis=0
        )
        back, arrived = exchanged(
            buffer, vectors, gate_w[0], up_w[0], down_w[0], activations
        )
        added = lax.dot_general(
            place_own, back.reshape(slots, width), (((0,), (0,)), ((), ())), preferred_element_type=jnp.float32
        )
        return (arrived.astype(jnp.float32) + added).astype(jnp.bfloat16)
    arrived = passed_along(activations, "section", 1)
    whole = lax.all_gather(
        jnp.concatenate([norm_gain, router[None, :]], axis=0), "expert", axis=1, tiled=True
    )
    rows = lax.all_to_all(buffer, "expert", split_axis=0, concat_axis=0, tiled=True)
    rows = rows.transpose(1, 0, 2).reshape(capacity, planes * width).astype(jnp.float32)
    image = lax.axis_index("expert") >= planes // 2
    gain = jnp.where(image, whole[1], whole[0])[None, :]
    scale = lax.rsqrt(jnp.sum(rows * rows, axis=1) / (planes * width) + EPS)
    score = jax.nn.sigmoid(scale * jnp.sum(rows * gain * whole[2][None, :], axis=1))
    normed = (rows * scale[:, None] * gain).astype(jnp.bfloat16)
    scores = lax.all_gather(passed_along(score, "section", 1), "expert", axis=0, tiled=True)
    block = lax.all_gather(normed, "section", axis=0, tiled=True)
    gate = feature_product(block, gate_w[0])
    upper = feature_product(block, up_w[0])
    hidden = (jax.nn.silu(gate) * upper).astype(jnp.bfloat16)
    hidden = jnp.roll(hidden, capacity, axis=0)
    part = jnp.dot(hidden, down_w[0], preferred_element_type=jnp.float32).astype(jnp.bfloat16)
    summed = lax.psum_scatter(part, "section", scatter_dimension=0, tiled=True)
    back = summed.reshape(capacity, planes, width).transpose(1, 0, 2)
    back = lax.all_to_all(back, "expert", split_axis=0, concat_axis=0, tiled=True)
    back = back.reshape(slots, width)
    high = scores.astype(jnp.bfloat16)
    low = (scores - high.astype(jnp.float32)).astype(jnp.bfloat16)
    spread = jnp.concatenate([place_own * high[:, None], place_own * low[:, None]], axis=0)
    added = lax.dot_general(
        spread,
        jnp.concatenate([back, back], axis=0),
        (((0,), (0,)), ((), ())),
        preferred_element_type=jnp.float32,
    )
    return (arrived.astype(jnp.float32) + added).astype(jnp.bfloat16)


def solution(mesh):
    placed = (
        P("section", "expert"),
        P("section"),
        P("section", None),
        P("section", None),
        P(None, "expert"),
        P("expert"),
        P("expert", "section", None),
        P("expert", "section", None),
        P("expert", "section", None),
    )
    return jax.shard_map(
        body, mesh=mesh, in_specs=placed, out_specs=P("section", "expert"), check_vma=False
    )
```

```python
import jax
import jax.numpy as jnp
from jax import lax
from jax.experimental import pallas as pl
from jax.experimental.pallas import tpu as pltpu
from jax.sharding import PartitionSpec as P

D = 8192


EPS = 1e-05


def passed_along(block, axis, distance):
    devices = range(lax.axis_size(axis))
    route = [((i - distance) % len(devices), i) for i in devices]
    return lax.ppermute(block, axis, route)


def feature_product(block, weight):
    return lax.dot_general(
        block, weight, (((1,), (1,)), ((), ())), preferred_element_type=jnp.float32
    )


def slot_map(picks, experts, capacity, slots, tokens):
    count = picks.shape[0]
    order = jnp.arange(count, dtype=jnp.int32)
    earlier = (experts[:, None] == experts[None, :]) & (order[None, :] < order[:, None])
    slot = jnp.sum(earlier.astype(jnp.int32), axis=1)
    target = experts * capacity + slot
    placing = (target[None, :] == jnp.arange(slots, dtype=jnp.int32)[:, None]).astype(jnp.bfloat16)
    picking = (picks[:, None] == jnp.arange(tokens, dtype=jnp.int32)[None, :]).astype(jnp.bfloat16)
    return jnp.dot(placing, picking, preferred_element_type=jnp.float32).astype(jnp.bfloat16)


LANES = 128
MESH = pl.DeviceIdType.MESH


def exchange_kernel(
    rows_in, vectors, gate_hbm, up_hbm, down_hbm, leaving, out, arrived,
    gate_v, up_v, down_v, came, vec, gathered, gate_sum, up_sum, hidden,
    for_sib, mine, from_sib, relay_x, relay_y, final_x, final_y, done,
    load_sem, z_send, z_recv, vec_send, vec_recv, ag_send, ag_recv, rs_send, rs_recv, back_send, back_recv,
    shift_send, shift_recv,
):
    planes, cap, width = rows_in.shape
    full = planes * width
    half = cap // 2
    hid = gate_hbm.shape[0]
    me, plane = lax.axis_index("section"), lax.axis_index("expert")
    core, chip = lax.rem(me, 2), lax.div(me, 2)
    x, y = lax.rem(chip, 2), lax.div(chip, 2)
    sib, xn, yn = me + 1 - 2 * core, me + 2 - 4 * x, me + 4 - 8 * y
    chip_x, chip_y = chip + 1 - 2 * x, chip + 2 - 4 * y
    chip_d = 3 - chip
    dests = {"x": (xn, plane), "y": (yn, plane), "s": (sib, plane)}
    uppers = [lax.rem(plane + j, planes) for j in range(1, planes)]

    sections = lax.axis_size("section")
    following, previous = lax.rem(me + 1, sections), lax.rem(me + sections - 1, sections)

    barrier = pltpu.get_barrier_semaphore()
    greeted = list(dests.values()) + [(me, p) for p in uppers]
    greeted += [(following, plane), (previous, plane)]
    for device in greeted:
        pl.semaphore_signal(barrier, inc=1, device_id=device, device_id_type=MESH)
    pl.semaphore_wait(barrier, len(greeted))

    sent = []

    def send(src, dst, send_sem, recv_sem, device):
        copy = pltpu.make_async_remote_copy(
            src_ref=src, dst_ref=dst, send_sem=send_sem, recv_sem=recv_sem,
            device_id=device, device_id_type=MESH,
        )
        copy.start()
        sent.append(copy)
        return copy

    early = leaving.shape[0] * 5 // 8
    parts = [pl.ds(0, early), pl.ds(early, leaving.shape[0] - early)]

    def shift(n):
        return send(
            leaving.at[parts[n]], arrived.at[parts[n]],
            shift_send.at[n], shift_recv.at[n], (following, plane),
        )

    z_copies = {}
    vec_copies = [
        send(vectors, vec.at[plane], vec_send.at[j], vec_recv.at[j], (me, p))
        for j, p in enumerate(uppers)
    ]

    def to_planes(part):
        piece = pl.ds(part * half, half)
        for j, p in enumerate(uppers):
            n = part * (planes - 1) + j
            z_copies[part, j] = send(
                rows_in.at[p, piece], came.at[plane, piece], z_send.at[n], z_recv.at[n], (me, p)
            )

    to_planes(0)
    shifts = [shift(0)]
    local = [
        pltpu.make_async_copy(rows_in.at[plane], came.at[plane], load_sem.at[0]),
        pltpu.make_async_copy(vectors, vec.at[plane], load_sem.at[1]),
        pltpu.make_async_copy(gate_hbm, gate_v, load_sem.at[2]),
        pltpu.make_async_copy(up_hbm, up_v, load_sem.at[3]),
        pltpu.make_async_copy(down_hbm, down_v, load_sem.at[4]),
    ]
    for copy in local:
        copy.start()
    for j in range(planes - 1):
        z_copies[0, j].wait_send()
    sent[:] = [copy for copy in sent if all(copy is not z_copies[0, j] for j in range(planes - 1))]
    to_planes(1)

    def place(owner_chip, owner_core, part):
        return pl.ds(
            pl.multiple_of((owner_chip * 2 + owner_core) * cap + part * half, 16), half
        )

    image = (plane >= planes // 2).astype(jnp.float32)

    def norm(part):
        @pl.loop(0, half // 16)
        def _(step):
            at = pl.ds(pl.multiple_of(part * half + step * 16, 16), 16)
            to = pl.ds(pl.multiple_of(me * cap + part * half + step * 16, 16), 16)
            squares = jnp.zeros((16, 1), jnp.float32)
            terms = jnp.zeros((16, 1), jnp.float32)
            for q in range(planes):
                rows = came[q, at, :].astype(jnp.float32)
                gain = vec[q, 0:1, :] * (1.0 - image) + vec[q, 1:2, :] * image
                squares += jnp.sum(rows * rows, axis=1, keepdims=True)
                terms += jnp.sum(rows * (gain * vec[q, 2:3, :]), axis=1, keepdims=True)
            scale = lax.rsqrt(squares / full + EPS)
            score = 1.0 / (1.0 + jnp.exp(-(scale * terms)))
            for q in range(planes):
                rows = came[q, at, :].astype(jnp.float32)
                gain = vec[q, 0:1, :] * (1.0 - image) + vec[q, 1:2, :] * image
                gathered[to, q * width : (q + 1) * width] = (rows * scale * gain).astype(jnp.bfloat16)
            high = jnp.broadcast_to(score, (16, LANES)).astype(jnp.bfloat16).astype(jnp.float32)
            lane = lax.broadcasted_iota(jnp.int32, (16, LANES), 1)
            gathered[to, full : full + LANES] = jnp.where(
                lane < LANES // 2, high, score - high
            ).astype(jnp.bfloat16)

    ag = {}
    names = ["x0", "x1", "y0", "y1", "fx", "fy", "s0", "s1", "sx0", "sx1", "sy0", "sy1", "sd0", "sd1"]

    def pass_block(name, owner_chip, part, to):
        ref = gathered.at[place(owner_chip, core, part)]
        n = names.index(name)
        ag[name] = send(ref, ref, ag_send.at[n], ag_recv.at[n], dests[to])

    local[0].wait()
    local[1].wait()
    for copy in vec_copies:
        copy.wait_recv()
    for part in range(2):
        for j in range(planes - 1):
            z_copies[part, j].wait_recv()
        norm(part)
        pass_block(f"x{part}", chip, part, "x")
        pass_block(f"y{part}", chip, part, "y")
        pass_block(f"s{part}", chip, part, "s")

    def products(owner_chip):
        first = pl.multiple_of(owner_chip * 2 * cap, 16)
        gate_sum[...] = jnp.zeros_like(gate_sum)
        up_sum[...] = jnp.zeros_like(up_sum)
        deep = 1024

        @pl.loop(0, full // deep)
        def _(step):
            columns = pl.ds(pl.multiple_of(step * deep, deep), deep)
            block = gathered[pl.ds(first, 2 * cap), columns]
            gate_sum[...] += feature_product(gate_v[:, columns], block)
            up_sum[...] += feature_product(up_v[:, columns], block)

        marks = gathered[pl.ds(first, 2 * cap), full : full + LANES].astype(jnp.float32)
        score = jnp.sum(marks, axis=1, keepdims=True) * (2.0 / LANES)
        gate = gate_sum[...]
        value = gate / (1.0 + jnp.exp(-gate)) * up_sum[...]
        value = (value.T * score).astype(jnp.bfloat16)
        hidden[1, pl.ds(pl.multiple_of(owner_chip * cap, 16), cap), :] = value[:cap]
        after = lax.rem(owner_chip + 1, 4)
        hidden[0, pl.ds(pl.multiple_of(after * cap, 16), cap), :] = value[cap:]

    ag["x0"].wait_recv()
    pass_block("fy", chip_x, 0, "y")
    pass_block("sx0", chip_x, 0, "s")
    ag["y0"].wait_recv()
    pass_block("sy0", chip_y, 0, "s")
    ag["s0"].wait_recv()
    ag["s1"].wait_recv()
    local[2].wait()
    local[3].wait()
    products(chip)
    ag["y1"].wait_recv()
    pass_block("fx", chip_y, 1, "x")
    pass_block("sy1", chip_y, 1, "s")
    ag["x1"].wait_recv()
    pass_block("sx1", chip_x, 1, "s")
    ag["sx0"].wait_recv()
    ag["sx1"].wait_recv()
    products(chip_x)
    ag["fy"].wait_recv()
    pass_block("sd0", chip_d, 0, "s")
    ag["sy0"].wait_recv()
    ag["sy1"].wait_recv()
    products(chip_y)
    ag["fx"].wait_recv()
    pass_block("sd1", chip_d, 1, "s")
    shifts.append(shift(1))
    ag["sd0"].wait_recv()
    ag["sd1"].wait_recv()
    products(chip_d)
    local[4].wait()

    rs = {}
    steps, span = mine.shape[0], mine.shape[2]
    halves = steps // planes
    targets = [lax.rem(plane + 1 + i // halves, planes) for i in range(steps)]

    def give(kind, n, i, src, dst, to):
        at = n * steps + i
        rs[kind, i] = send(src, dst, rs_send.at[at], rs_recv.at[at], dests[to])

    def down(i, which, into):
        wide = 512

        @pl.loop(0, span // wide)
        def _(step):
            start = targets[i] * width + i % halves * span + step * wide
            columns = pl.ds(pl.multiple_of(start, wide), wide)
            to = pl.ds(pl.multiple_of(step * wide, wide), wide)
            into[i, :, to] = jnp.dot(
                hidden[which], down_v[:, columns], preferred_element_type=jnp.float32
            ).astype(jnp.bfloat16)

    def start_sums(i):
        down(i, 1 - core, for_sib)
        give("s", 0, i, for_sib.at[i], from_sib.at[i], "s")

    def own_sums(i):
        down(i, core, mine)

    def add_into(ref, i, first, count, others):
        @pl.loop(0, count // 16)
        def _(step):
            at = pl.ds(pl.multiple_of(first + step * 16, 16), 16)
            total = mine[i, at, :].astype(jnp.float32)
            for other, begin in others:
                rows = pl.ds(pl.multiple_of(begin + step * 16, 16), 16)
                total += other[i, rows, :].astype(jnp.float32)
            if ref is None:
                mine[i, at, :] = total.astype(jnp.bfloat16)
            else:
                ref[i, pl.ds(pl.multiple_of(step * 16, 16), 16), :] = total.astype(jnp.bfloat16)

    def chip_sums(i):
        rs["s", i].wait_recv()
        for other in (chip_d, chip_x, chip_y):
            base = pl.multiple_of(other * cap, 16)
            add_into(None, i, base, cap, [(from_sib, base)])
            low, high = pl.ds(base, half), pl.ds(pl.multiple_of(base + half, 16), half)
            if other is chip_d:
                give("rx", 1, i, mine.at[i, low], relay_x.at[i], "x")
                give("ry", 2, i, mine.at[i, high], relay_y.at[i], "y")
            elif other is chip_x:
                give("x0", 3, i, mine.at[i, low], final_x.at[i, pl.ds(0, half)], "x")
            else:
                give("y1", 4, i, mine.at[i, high], final_y.at[i, pl.ds(half, half)], "y")

    def relay_sums(i):
        rs["rx", i].wait_recv()
        first = pl.multiple_of(chip_y * cap, 16)
        add_into(None, i, first, half, [(relay_x, 0)])
        give("y0", 5, i, mine.at[i, pl.ds(first, half)], final_y.at[i, pl.ds(0, half)], "y")
        rs["ry", i].wait_recv()
        first = pl.multiple_of(chip_x * cap + half, 16)
        add_into(None, i, first, half, [(relay_y, 0)])
        give("x1", 6, i, mine.at[i, pl.ds(first, half)], final_x.at[i, pl.ds(half, half)], "x")

    back, own = [], []

    def final_sums(i):
        for kind in ("x0", "y1", "y0", "x1"):
            rs[kind, i].wait_recv()
        base = pl.multiple_of(chip * cap, 16)
        add_into(done, i, base, cap, [(from_sib, base), (final_x, 0), (final_y, 0)])
        to = out.at[plane, :, pl.ds(i % halves * span, span)]
        if i < steps - halves:
            back.append(send(done.at[i], to, back_send.at[i], back_recv.at[i], (me, targets[i])))
        else:
            copy = pltpu.make_async_copy(done.at[i], to, load_sem.at[5 + i - (steps - halves)])
            copy.start()
            own.append(copy)

    start_sums(0)
    own_sums(0)
    for i in range(steps + 3):
        if i + 1 < steps:
            start_sums(i + 1)
        if i < steps:
            chip_sums(i)
        if i + 1 < steps:
            own_sums(i + 1)
        if 0 <= i - 2 < steps:
            relay_sums(i - 2)
        if 0 <= i - 3 < steps:
            final_sums(i - 3)
    for copy in back:
        copy.wait_recv()
    for copy in own:
        copy.wait()
    for copy in shifts:
        copy.wait_recv()
    for copy in sent:
        copy.wait_send()


def exchanged(buffer, vectors, gate, up, down, leaving):
    planes, cap, width = buffer.shape
    hid, full = gate.shape
    half, chips, halves = cap // 2, 4, 2
    steps, span = planes * halves, width // halves
    bf, dma = jnp.bfloat16, pltpu.SemaphoreType.DMA
    anywhere = pl.BlockSpec(memory_space=pl.ANY)
    return pl.pallas_call(
        exchange_kernel,
        out_shape=[
            jax.ShapeDtypeStruct(buffer.shape, bf),
            jax.ShapeDtypeStruct(leaving.shape, bf),
        ],
        in_specs=[anywhere] * 6,
        out_specs=[anywhere] * 2,
        scratch_shapes=[
            pltpu.VMEM((hid, full), bf),
            pltpu.VMEM((hid, full), bf),
            pltpu.VMEM((hid, full), bf),
            pltpu.VMEM((planes, cap, width), bf),
            pltpu.VMEM((planes,) + vectors.shape, jnp.float32),
            pltpu.VMEM((2 * chips * cap, full + LANES), bf),
            pltpu.VMEM((hid, 2 * cap), jnp.float32),
            pltpu.VMEM((hid, 2 * cap), jnp.float32),
            pltpu.VMEM((2, chips * cap, hid), bf),
            pltpu.VMEM((steps, chips * cap, span), bf),
            pltpu.VMEM((steps, chips * cap, span), bf),
            pltpu.VMEM((steps, chips * cap, span), bf),
            pltpu.VMEM((steps, half, span), bf),
            pltpu.VMEM((steps, half, span), bf),
            pltpu.VMEM((steps, cap, span), bf),
            pltpu.VMEM((steps, cap, span), bf),
            pltpu.VMEM((steps, cap, span), bf),
            dma((5 + halves,)),
            dma((2 * (planes - 1),)),
            dma((2 * (planes - 1),)),
            dma((planes - 1,)),
            dma((planes - 1,)),
            dma((14,)),
            dma((14,)),
            dma((7 * steps,)),
            dma((7 * steps,)),
            dma((steps - halves,)),
            dma((steps - halves,)),
            dma((2,)),
            dma((2,)),
        ],
        compiler_params=pltpu.CompilerParams(
            collective_id=0, has_side_effects=True, vmem_limit_bytes=63 * 1024 * 1024
        ),
        cost_estimate=pl.CostEstimate(
            flops=6 * 2 * chips * cap * hid * full, bytes_accessed=6 * hid * full, transcendentals=0
        ),
    )(buffer, vectors, gate, up, down, leaving)


def body(activations, modality, selected, routes, norm_gain, router, gate_w, up_w, down_w):
    sections, planes = lax.axis_size("section"), lax.axis_size("expert")
    tokens, width = activations.shape
    picks, experts = selected[0], routes[:, 0]
    expert_count = planes * gate_w.shape[0]
    capacity = max(2, 3 * picks.shape[0] // (2 * expert_count))
    slots = expert_count * capacity
    ahead = passed_along(jnp.stack([picks, experts]), "section", -1)
    place_own = lax.optimization_barrier(slot_map(picks, experts, capacity, slots, tokens))
    place_ahead = lax.optimization_barrier(
        slot_map(ahead[0], ahead[1], capacity, slots, tokens)
    )
    buffer = jnp.dot(place_ahead, activations, preferred_element_type=jnp.float32)
    buffer = buffer.astype(jnp.bfloat16).reshape(planes, capacity, width)
    if (sections, planes) == (8, 4) and capacity % 32 == 0:
        vectors = jnp.concatenate(
            [norm_gain, router[None, :], jnp.zeros((5, width), jnp.float32)], axis=0
        )
        back, arrived = exchanged(
            buffer, vectors, gate_w[0], up_w[0], down_w[0], activations
        )
        added = lax.dot_general(
            place_own, back.reshape(slots, width), (((0,), (0,)), ((), ())), preferred_element_type=jnp.float32
        )
        return (arrived.astype(jnp.float32) + added).astype(jnp.bfloat16)
    arrived = passed_along(activations, "section", 1)
    whole = lax.all_gather(
        jnp.concatenate([norm_gain, router[None, :]], axis=0), "expert", axis=1, tiled=True
    )
    rows = lax.all_to_all(buffer, "expert", split_axis=0, concat_axis=0, tiled=True)
    rows = rows.transpose(1, 0, 2).reshape(capacity, planes * width).astype(jnp.float32)
    image = lax.axis_index("expert") >= planes // 2
    gain = jnp.where(image, whole[1], whole[0])[None, :]
    scale = lax.rsqrt(jnp.sum(rows * rows, axis=1) / (planes * width) + EPS)
    score = jax.nn.sigmoid(scale * jnp.sum(rows * gain * whole[2][None, :], axis=1))
    normed = (rows * scale[:, None] * gain).astype(jnp.bfloat16)
    scores = lax.all_gather(passed_along(score, "section", 1), "expert", axis=0, tiled=True)
    block = lax.all_gather(normed, "section", axis=0, tiled=True)
    gate = feature_product(block, gate_w[0])
    upper = feature_product(block, up_w[0])
    hidden = (jax.nn.silu(gate) * upper).astype(jnp.bfloat16)
    hidden = jnp.roll(hidden, capacity, axis=0)
    part = jnp.dot(hidden, down_w[0], preferred_element_type=jnp.float32).astype(jnp.bfloat16)
    summed = lax.psum_scatter(part, "section", scatter_dimension=0, tiled=True)
    back = summed.reshape(capacity, planes, width).transpose(1, 0, 2)
    back = lax.all_to_all(back, "expert", split_axis=0, concat_axis=0, tiled=True)
    back = back.reshape(slots, width)
    high = scores.astype(jnp.bfloat16)
    low = (scores - high.astype(jnp.float32)).astype(jnp.bfloat16)
    spread = jnp.concatenate([place_own * high[:, None], place_own * low[:, None]], axis=0)
    added = lax.dot_general(
        spread,
        jnp.concatenate([back, back], axis=0),
        (((0,), (0,)), ((), ())),
        preferred_element_type=jnp.float32,
    )
    return (arrived.astype(jnp.float32) + added).astype(jnp.bfloat16)


def solution(mesh):
    placed = (
        P("section", "expert"),
        P("section"),
        P("section", None),
        P("section", None),
        P(None, "expert"),
        P("expert"),
        P("expert", "section", None),
        P("expert", "section", None),
        P("expert", "section", None),
    )
    return jax.shard_map(
        body, mesh=mesh, in_specs=placed, out_specs=P("section", "expert"), check_vma=False
    )
```

```python
import jax
import jax.numpy as jnp
from jax import lax
from jax.experimental import pallas as pl
from jax.experimental.pallas import tpu as pltpu
from jax.sharding import PartitionSpec as P

D = 8192


EPS = 1e-05


def passed_along(block, axis, distance):
    devices = range(lax.axis_size(axis))
    route = [((i - distance) % len(devices), i) for i in devices]
    return lax.ppermute(block, axis, route)


def feature_product(block, weight):
    return lax.dot_general(
        block, weight, (((1,), (1,)), ((), ())), preferred_element_type=jnp.float32
    )


def slot_map(picks, experts, capacity, slots, tokens):
    count = picks.shape[0]
    order = jnp.arange(count, dtype=jnp.int32)
    earlier = (experts[:, None] == experts[None, :]) & (order[None, :] < order[:, None])
    slot = jnp.sum(earlier.astype(jnp.int32), axis=1)
    target = experts * capacity + slot
    placing = (target[None, :] == jnp.arange(slots, dtype=jnp.int32)[:, None]).astype(jnp.bfloat16)
    picking = (picks[:, None] == jnp.arange(tokens, dtype=jnp.int32)[None, :]).astype(jnp.bfloat16)
    return jnp.dot(placing, picking, preferred_element_type=jnp.float32).astype(jnp.bfloat16)


LANES = 128
MESH = pl.DeviceIdType.MESH


def exchange_kernel(
    rows_in, vectors, gate_hbm, up_hbm, down_hbm, leaving, out, arrived,
    gate_v, up_v, down_v, came, vec, gathered, gate_sum, up_sum, hidden,
    for_sib, mine, from_sib, relay_x, relay_y, final_x, final_y, done,
    load_sem, z_send, z_recv, vec_send, vec_recv, ag_send, ag_recv, rs_send, rs_recv, back_send, back_recv,
    shift_send, shift_recv,
):
    planes, cap, width = rows_in.shape
    full = planes * width
    half = cap // 2
    thin = 16
    pieces = cap // thin
    hid = gate_hbm.shape[0]
    me, plane = lax.axis_index("section"), lax.axis_index("expert")
    core, chip = lax.rem(me, 2), lax.div(me, 2)
    x, y = lax.rem(chip, 2), lax.div(chip, 2)
    sib, xn, yn = me + 1 - 2 * core, me + 2 - 4 * x, me + 4 - 8 * y
    chip_x, chip_y = chip + 1 - 2 * x, chip + 2 - 4 * y
    chip_d = 3 - chip
    dests = {"x": (xn, plane), "y": (yn, plane), "s": (sib, plane)}
    uppers = [lax.rem(plane + j, planes) for j in range(1, planes)]

    sections = lax.axis_size("section")
    following, previous = lax.rem(me + 1, sections), lax.rem(me + sections - 1, sections)

    barrier = pltpu.get_barrier_semaphore()
    greeted = list(dests.values()) + [(me, p) for p in uppers]
    greeted += [(following, plane), (previous, plane)]
    for device in greeted:
        pl.semaphore_signal(barrier, inc=1, device_id=device, device_id_type=MESH)
    pl.semaphore_wait(barrier, len(greeted))

    sent = []

    def send(src, dst, send_sem, recv_sem, device):
        copy = pltpu.make_async_remote_copy(
            src_ref=src, dst_ref=dst, send_sem=send_sem, recv_sem=recv_sem,
            device_id=device, device_id_type=MESH,
        )
        copy.start()
        sent.append(copy)
        return copy

    early = leaving.shape[0] * 5 // 8
    parts = [pl.ds(0, early), pl.ds(early, leaving.shape[0] - early)]

    def shift(n):
        return send(
            leaving.at[parts[n]], arrived.at[parts[n]],
            shift_send.at[n], shift_recv.at[n], (following, plane),
        )

    z_copies = {}
    vec_copies = [
        send(vectors, vec.at[plane], vec_send.at[j], vec_recv.at[j], (me, p))
        for j, p in enumerate(uppers)
    ]

    def to_planes(part):
        piece = pl.ds(part * thin, thin)
        for j, p in enumerate(uppers):
            n = part * (planes - 1) + j
            z_copies[part, j] = send(
                rows_in.at[p, piece], came.at[plane, piece], z_send.at[n], z_recv.at[n], (me, p)
            )

    to_planes(0)
    shifts = [shift(0)]
    local = [
        pltpu.make_async_copy(rows_in.at[plane], came.at[plane], load_sem.at[0]),
        pltpu.make_async_copy(vectors, vec.at[plane], load_sem.at[1]),
        pltpu.make_async_copy(gate_hbm, gate_v, load_sem.at[2]),
        pltpu.make_async_copy(up_hbm, up_v, load_sem.at[3]),
        pltpu.make_async_copy(down_hbm, down_v, load_sem.at[4]),
    ]
    for copy in local:
        copy.start()

    def place(owner_chip, owner_core, part):
        return pl.ds(
            pl.multiple_of((owner_chip * 2 + owner_core) * cap + part * thin, 16), thin
        )

    image = (plane >= planes // 2).astype(jnp.float32)

    def norm(part):
        @pl.loop(0, thin // 16)
        def _(step):
            at = pl.ds(pl.multiple_of(part * thin + step * 16, 16), 16)
            to = pl.ds(pl.multiple_of(me * cap + part * thin + step * 16, 16), 16)
            squares = jnp.zeros((16, 1), jnp.float32)
            terms = jnp.zeros((16, 1), jnp.float32)
            for q in range(planes):
                rows = came[q, at, :].astype(jnp.float32)
                gain = vec[q, 0:1, :] * (1.0 - image) + vec[q, 1:2, :] * image
                squares += jnp.sum(rows * rows, axis=1, keepdims=True)
                terms += jnp.sum(rows * (gain * vec[q, 2:3, :]), axis=1, keepdims=True)
            scale = lax.rsqrt(squares / full + EPS)
            score = 1.0 / (1.0 + jnp.exp(-(scale * terms)))
            for q in range(planes):
                rows = came[q, at, :].astype(jnp.float32)
                gain = vec[q, 0:1, :] * (1.0 - image) + vec[q, 1:2, :] * image
                gathered[to, q * width : (q + 1) * width] = (rows * scale * gain).astype(jnp.bfloat16)
            high = jnp.broadcast_to(score, (16, LANES)).astype(jnp.bfloat16).astype(jnp.float32)
            lane = lax.broadcasted_iota(jnp.int32, (16, LANES), 1)
            gathered[to, full : full + LANES] = jnp.where(
                lane < LANES // 2, high, score - high
            ).astype(jnp.bfloat16)

    ag = {}
    kinds = ["x", "y", "f", "s", "sx", "sy", "sd"]

    def pass_block(kind, owner_chip, part, to):
        ref = gathered.at[place(owner_chip, core, part)]
        n = kinds.index(kind) * pieces + part
        ag[kind, part] = send(ref, ref, ag_send.at[n], ag_recv.at[n], dests[to])

    local[0].wait()
    local[1].wait()
    for copy in vec_copies:
        copy.wait_recv()

    def forward(part):
        ag["x", part].wait_recv()
        if part % 2 == 0:
            pass_block("f", chip_x, part, "y")
        pass_block("sx", chip_x, part, "s")
        ag["y", part].wait_recv()
        if part % 2 == 1:
            pass_block("f", chip_y, part, "x")
        pass_block("sy", chip_y, part, "s")

    def forward_last(part):
        ag["f", part].wait_recv()
        pass_block("sd", chip_d, part, "s")

    def wait_all(kind):
        for part in range(pieces):
            ag[kind, part].wait_recv()

    for part in range(pieces):
        for j in range(planes - 1):
            z_copies[part, j].wait_send()
        if part + 1 < pieces:
            to_planes(part + 1)
        for j in range(planes - 1):
            z_copies[part, j].wait_recv()
        norm(part)
        pass_block("x", chip, part, "x")
        pass_block("y", chip, part, "y")
        pass_block("s", chip, part, "s")
        if part >= 1:
            forward(part - 1)
    forward(pieces - 1)
    gone = [id(copy) for copy in z_copies.values()]
    sent[:] = [copy for copy in sent if id(copy) not in gone]

    def products(owner_chip):
        first = pl.multiple_of(owner_chip * 2 * cap, 16)
        gate_sum[...] = jnp.zeros_like(gate_sum)
        up_sum[...] = jnp.zeros_like(up_sum)
        deep = 1024

        @pl.loop(0, full // deep)
        def _(step):
            columns = pl.ds(pl.multiple_of(step * deep, deep), deep)
            block = gathered[pl.ds(first, 2 * cap), columns]
            gate_sum[...] += feature_product(gate_v[:, columns], block)
            up_sum[...] += feature_product(up_v[:, columns], block)

        marks = gathered[pl.ds(first, 2 * cap), full : full + LANES].astype(jnp.float32)
        score = jnp.sum(marks, axis=1, keepdims=True) * (2.0 / LANES)
        gate = gate_sum[...]
        value = gate / (1.0 + jnp.exp(-gate)) * up_sum[...]
        value = (value.T * score).astype(jnp.bfloat16)
        hidden[1, pl.ds(pl.multiple_of(owner_chip * cap, 16), cap), :] = value[:cap]
        after = lax.rem(owner_chip + 1, 4)
        hidden[0, pl.ds(pl.multiple_of(after * cap, 16), cap), :] = value[cap:]

    wait_all("s")
    local[2].wait()
    local[3].wait()
    products(chip)
    for part in range(pieces - 2):
        forward_last(part)
    wait_all("sx")
    products(chip_x)
    forward_last(pieces - 2)
    wait_all("sy")
    products(chip_y)
    forward_last(pieces - 1)
    shifts.append(shift(1))
    wait_all("sd")
    products(chip_d)
    local[4].wait()

    rs = {}
    steps, span = mine.shape[0], mine.shape[2]
    halves = steps // planes
    targets = [lax.rem(plane + 1 + i // halves, planes) for i in range(steps)]

    def give(kind, n, i, src, dst, to):
        at = n * steps + i
        rs[kind, i] = send(src, dst, rs_send.at[at], rs_recv.at[at], dests[to])

    def down(i, which, into):
        wide = 512

        @pl.loop(0, span // wide)
        def _(step):
            start = targets[i] * width + i % halves * span + step * wide
            columns = pl.ds(pl.multiple_of(start, wide), wide)
            to = pl.ds(pl.multiple_of(step * wide, wide), wide)
            into[i, :, to] = jnp.dot(
                hidden[which], down_v[:, columns], preferred_element_type=jnp.float32
            ).astype(jnp.bfloat16)

    def start_sums(i):
        down(i, 1 - core, for_sib)
        give("s", 0, i, for_sib.at[i], from_sib.at[i], "s")

    def own_sums(i):
        down(i, core, mine)

    def add_into(ref, i, first, count, others):
        @pl.loop(0, count // 16)
        def _(step):
            at = pl.ds(pl.multiple_of(first + step * 16, 16), 16)
            total = mine[i, at, :].astype(jnp.float32)
            for other, begin in others:
                rows = pl.ds(pl.multiple_of(begin + step * 16, 16), 16)
                total += other[i, rows, :].astype(jnp.float32)
            if ref is None:
                mine[i, at, :] = total.astype(jnp.bfloat16)
            else:
                ref[i, pl.ds(pl.multiple_of(step * 16, 16), 16), :] = total.astype(jnp.bfloat16)

    def chip_sums(i):
        rs["s", i].wait_recv()
        for other in (chip_d, chip_x, chip_y):
            base = pl.multiple_of(other * cap, 16)
            add_into(None, i, base, cap, [(from_sib, base)])
            low, high = pl.ds(base, half), pl.ds(pl.multiple_of(base + half, 16), half)
            if other is chip_d:
                give("rx", 1, i, mine.at[i, low], relay_x.at[i], "x")
                give("ry", 2, i, mine.at[i, high], relay_y.at[i], "y")
            elif other is chip_x:
                give("x0", 3, i, mine.at[i, low], final_x.at[i, pl.ds(0, half)], "x")
            else:
                give("y1", 4, i, mine.at[i, high], final_y.at[i, pl.ds(half, half)], "y")

    def relay_sums(i):
        rs["rx", i].wait_recv()
        first = pl.multiple_of(chip_y * cap, 16)
        add_into(None, i, first, half, [(relay_x, 0)])
        give("y0", 5, i, mine.at[i, pl.ds(first, half)], final_y.at[i, pl.ds(0, half)], "y")
        rs["ry", i].wait_recv()
        first = pl.multiple_of(chip_x * cap + half, 16)
        add_into(None, i, first, half, [(relay_y, 0)])
        give("x1", 6, i, mine.at[i, pl.ds(first, half)], final_x.at[i, pl.ds(half, half)], "x")

    back, own = [], []

    def final_sums(i):
        for kind in ("x0", "y1", "y0", "x1"):
            rs[kind, i].wait_recv()
        base = pl.multiple_of(chip * cap, 16)
        add_into(done, i, base, cap, [(from_sib, base), (final_x, 0), (final_y, 0)])
        to = out.at[plane, :, pl.ds(i % halves * span, span)]
        if i < steps - halves:
            back.append(send(done.at[i], to, back_send.at[i], back_recv.at[i], (me, targets[i])))
        else:
            copy = pltpu.make_async_copy(done.at[i], to, load_sem.at[5 + i - (steps - halves)])
            copy.start()
            own.append(copy)

    start_sums(0)
    own_sums(0)
    for i in range(steps + 3):
        if i + 1 < steps:
            start_sums(i + 1)
        if i < steps:
            chip_sums(i)
        if i + 1 < steps:
            own_sums(i + 1)
        if 0 <= i - 2 < steps:
            relay_sums(i - 2)
        if 0 <= i - 3 < steps:
            final_sums(i - 3)
    for copy in back:
        copy.wait_recv()
    for copy in own:
        copy.wait()
    for copy in shifts:
        copy.wait_recv()
    for copy in sent:
        copy.wait_send()


def exchanged(buffer, vectors, gate, up, down, leaving):
    planes, cap, width = buffer.shape
    hid, full = gate.shape
    half, chips, halves = cap // 2, 4, 2
    steps, span = planes * halves, width // halves
    bf, dma = jnp.bfloat16, pltpu.SemaphoreType.DMA
    anywhere = pl.BlockSpec(memory_space=pl.ANY)
    return pl.pallas_call(
        exchange_kernel,
        out_shape=[
            jax.ShapeDtypeStruct(buffer.shape, bf),
            jax.ShapeDtypeStruct(leaving.shape, bf),
        ],
        in_specs=[anywhere] * 6,
        out_specs=[anywhere] * 2,
        scratch_shapes=[
            pltpu.VMEM((hid, full), bf),
            pltpu.VMEM((hid, full), bf),
            pltpu.VMEM((hid, full), bf),
            pltpu.VMEM((planes, cap, width), bf),
            pltpu.VMEM((planes,) + vectors.shape, jnp.float32),
            pltpu.VMEM((2 * chips * cap, full + LANES), bf),
            pltpu.VMEM((hid, 2 * cap), jnp.float32),
            pltpu.VMEM((hid, 2 * cap), jnp.float32),
            pltpu.VMEM((2, chips * cap, hid), bf),
            pltpu.VMEM((steps, chips * cap, span), bf),
            pltpu.VMEM((steps, chips * cap, span), bf),
            pltpu.VMEM((steps, chips * cap, span), bf),
            pltpu.VMEM((steps, half, span), bf),
            pltpu.VMEM((steps, half, span), bf),
            pltpu.VMEM((steps, cap, span), bf),
            pltpu.VMEM((steps, cap, span), bf),
            pltpu.VMEM((steps, cap, span), bf),
            dma((5 + halves,)),
            dma((cap // 16 * (planes - 1),)),
            dma((cap // 16 * (planes - 1),)),
            dma((planes - 1,)),
            dma((planes - 1,)),
            dma((7 * cap // 16,)),
            dma((7 * cap // 16,)),
            dma((7 * steps,)),
            dma((7 * steps,)),
            dma((steps - halves,)),
            dma((steps - halves,)),
            dma((2,)),
            dma((2,)),
        ],
        compiler_params=pltpu.CompilerParams(
            collective_id=0, has_side_effects=True, vmem_limit_bytes=63 * 1024 * 1024
        ),
        cost_estimate=pl.CostEstimate(
            flops=6 * 2 * chips * cap * hid * full, bytes_accessed=6 * hid * full, transcendentals=0
        ),
    )(buffer, vectors, gate, up, down, leaving)


def body(activations, modality, selected, routes, norm_gain, router, gate_w, up_w, down_w):
    sections, planes = lax.axis_size("section"), lax.axis_size("expert")
    tokens, width = activations.shape
    picks, experts = selected[0], routes[:, 0]
    expert_count = planes * gate_w.shape[0]
    capacity = max(2, 3 * picks.shape[0] // (2 * expert_count))
    slots = expert_count * capacity
    ahead = passed_along(jnp.stack([picks, experts]), "section", -1)
    place_own = lax.optimization_barrier(slot_map(picks, experts, capacity, slots, tokens))
    place_ahead = lax.optimization_barrier(
        slot_map(ahead[0], ahead[1], capacity, slots, tokens)
    )
    buffer = jnp.dot(place_ahead, activations, preferred_element_type=jnp.float32)
    buffer = buffer.astype(jnp.bfloat16).reshape(planes, capacity, width)
    if (sections, planes) == (8, 4) and capacity % 32 == 0:
        vectors = jnp.concatenate(
            [norm_gain, router[None, :], jnp.zeros((5, width), jnp.float32)], axis=0
        )
        back, arrived = exchanged(
            buffer, vectors, gate_w[0], up_w[0], down_w[0], activations
        )
        added = lax.dot_general(
            place_own, back.reshape(slots, width), (((0,), (0,)), ((), ())), preferred_element_type=jnp.float32
        )
        return (arrived.astype(jnp.float32) + added).astype(jnp.bfloat16)
    arrived = passed_along(activations, "section", 1)
    whole = lax.all_gather(
        jnp.concatenate([norm_gain, router[None, :]], axis=0), "expert", axis=1, tiled=True
    )
    rows = lax.all_to_all(buffer, "expert", split_axis=0, concat_axis=0, tiled=True)
    rows = rows.transpose(1, 0, 2).reshape(capacity, planes * width).astype(jnp.float32)
    image = lax.axis_index("expert") >= planes // 2
    gain = jnp.where(image, whole[1], whole[0])[None, :]
    scale = lax.rsqrt(jnp.sum(rows * rows, axis=1) / (planes * width) + EPS)
    score = jax.nn.sigmoid(scale * jnp.sum(rows * gain * whole[2][None, :], axis=1))
    normed = (rows * scale[:, None] * gain).astype(jnp.bfloat16)
    scores = lax.all_gather(passed_along(score, "section", 1), "expert", axis=0, tiled=True)
    block = lax.all_gather(normed, "section", axis=0, tiled=True)
    gate = feature_product(block, gate_w[0])
    upper = feature_product(block, up_w[0])
    hidden = (jax.nn.silu(gate) * upper).astype(jnp.bfloat16)
    hidden = jnp.roll(hidden, capacity, axis=0)
    part = jnp.dot(hidden, down_w[0], preferred_element_type=jnp.float32).astype(jnp.bfloat16)
    summed = lax.psum_scatter(part, "section", scatter_dimension=0, tiled=True)
    back = summed.reshape(capacity, planes, width).transpose(1, 0, 2)
    back = lax.all_to_all(back, "expert", split_axis=0, concat_axis=0, tiled=True)
    back = back.reshape(slots, width)
    high = scores.astype(jnp.bfloat16)
    low = (scores - high.astype(jnp.float32)).astype(jnp.bfloat16)
    spread = jnp.concatenate([place_own * high[:, None], place_own * low[:, None]], axis=0)
    added = lax.dot_general(
        spread,
        jnp.concatenate([back, back], axis=0),
        (((0,), (0,)), ((), ())),
        preferred_element_type=jnp.float32,
    )
    return (arrived.astype(jnp.float32) + added).astype(jnp.bfloat16)


def solution(mesh):
    placed = (
        P("section", "expert"),
        P("section"),
        P("section", None),
        P("section", None),
        P(None, "expert"),
        P("expert"),
        P("expert", "section", None),
        P("expert", "section", None),
        P("expert", "section", None),
    )
    return jax.shard_map(
        body, mesh=mesh, in_specs=placed, out_specs=P("section", "expert"), check_vma=False
    )
```
